128 devices in a mesh: tower: 16 (over z, x_lo, core), dev: 8 (over x_hi, y).
Axes of the slice: x: 4 (x_hi: 2, x_lo: 2; x = x_hi * 2 + x_lo), y: 4, z: 4, core: 2. Of those that a mesh axis runs over, the one named last changes fastest.
Arguments:
- embeddings: bfloat16 [8192, 32768], P(None, ('tower', 'dev')), may hold values from -6 to 6
- tower_v: bfloat16 [16, 2048, 256], P('tower'), may hold values from -0.125 to 0.125
- tower_u: bfloat16 [16, 256, 2048], P('tower'), may hold values from -0.375 to 0.375
- cross_bias: float32 [16, 2048], P('tower'), may hold values from -3 to 3
- proj_w: bfloat16 [16, 2048, 128], P('tower'), may hold values from -0.125 to 0.125
- proj_bias: float32 [16, 128], P('tower'), may hold values from -3 to 3
- arch_v: bfloat16 [2048, 512], replicated, may hold values from -0.125 to 0.125
- arch_u: bfloat16 [512, 2048], replicated, may hold values from -0.25 to 0.25
- arch_bias: float32 [2048], replicated, may hold values from -3 to 3
- logit_w: float32 [2048], replicated, may hold values from -0.125 to 0.125
- labels: float32 [8192], P(('tower', 'dev')), may hold values from 0 to 1
Outputs:
- emb_grad: bfloat16 [8192, 32768], P(None, ('tower', 'dev'))
- grad_tower_v: float32 [16, 2048, 256], P('tower', 'dev')
- grad_tower_u: float32 [16, 256, 2048], P('tower', 'dev')
- grad_cross_bias: float32 [16, 2048], P('tower', 'dev')
- grad_proj_w: float32 [16, 2048, 128], P('tower', 'dev')
- grad_proj_bias: float32 [16, 128], P('tower', 'dev')
- grad_arch_v: float32 [2048, 512], P(('tower', 'dev'))
- grad_arch_u: float32 [512, 2048], P(('tower', 'dev'))
- grad_arch_bias: float32 [2048], P(('tower', 'dev'))
- grad_logit_w: float32 [2048], P(('tower', 'dev'))
The draws below stay inside these ranges and needn't reach their ends.
All inputs are finite; a program needn't handle non-finite values.
Results may differ from the reference program's by a relative error of at most 0.025.
Values may be sent and summed in bfloat16 or wider, within the bound.
A program may use at most 128 MiB of HBM per device.

```python
import jax
import jax.numpy as jnp
from jax import lax

RANK = 256
PROJ = 128
ARCH_RANK = 512
LOSS_SCALE = 1024
TW = 2048
ARCH = 2048
TOKENS = 8192
N_TOWER = 16


def shard_levels(rng, extent, cuts, low, top_value):
    factor_of = 1.0
    for axis_at, shards_of in cuts:
        heights = jax.random.uniform(jax.random.fold_in(jax.random.fold_in(rng, 6), axis_at), (shards_of,), jnp.float32, low / len(cuts), top_value / len(cuts))
        factor_of = factor_of * jnp.repeat(jnp.exp(heights), extent[axis_at] // shards_of).reshape((-1,) + (1,) * (len(extent) - 1 - axis_at))
    return factor_of


def centred(own_key, shape, scale, bound, shards=(), kind=jnp.bfloat16):
    drawn = scale * jax.random.normal(own_key, shape, jnp.float32)
    if shards:
        drawn = drawn * shard_levels(own_key, shape, shards, -0.22, 0.18)
    return jnp.clip(drawn, -bound, bound).astype(kind)


def setup_inputs(seed: int = 0) -> dict:
    seeds = jax.random.split(jax.random.key(seed), 12)
    embeddings = centred(seeds[0], (TOKENS, N_TOWER * TW), 1.0, 6.0, ((1, 128),))
    tower_v = centred(seeds[1], (N_TOWER, TW, RANK), TW ** -0.5, 0.125, ((0, 16),))
    tower_u = centred(seeds[2], (N_TOWER, RANK, TW), RANK ** -0.5, 0.375, ((0, 16),))
    cross_bias = centred(seeds[3], (N_TOWER, TW), 0.5, 3.0, ((0, 16),), jnp.float32)
    proj_w = centred(seeds[4], (N_TOWER, TW, PROJ), TW ** -0.5, 0.125, ((0, 16),))
    proj_bias = centred(seeds[5], (N_TOWER, PROJ), 0.5, 3.0, ((0, 16),), jnp.float32)
    arch_v = centred(seeds[6], (ARCH, ARCH_RANK), ARCH ** -0.5, 0.125)
    arch_u = centred(seeds[7], (ARCH_RANK, ARCH), ARCH_RANK ** -0.5, 0.25)
    arch_bias = centred(seeds[8], (ARCH,), 0.5, 3.0, (), jnp.float32)
    logit_w = centred(seeds[9], (ARCH,), ARCH ** -0.5, 0.125, (), jnp.float32)
    labels = jnp.clip(1.0 * jax.random.uniform(seeds[10], (TOKENS,), jnp.float32) ** shard_levels(seeds[10], (TOKENS,), ((0, 128),), -0.2, 0.2), 0.0, 1.0)
    return {"embeddings": embeddings, "tower_v": tower_v, "tower_u": tower_u, "cross_bias": cross_bias, "proj_w": proj_w, "proj_bias": proj_bias, "arch_v": arch_v, "arch_u": arch_u, "arch_bias": arch_bias, "logit_w": logit_w, "labels": labels}


def inner_rows(left, right):
    return lax.dot_general(left, right, (((0,), (0,)), ((), ())), preferred_element_type=jnp.float32)

def outer_cols(left, right):
    return lax.dot_general(left, right, (((1,), (1,)), ((), ())), preferred_element_type=jnp.float32)

def silu_grad(values):
    sigmas = jax.nn.sigmoid(values)
    return sigmas * (1.0 + values * (1.0 - sigmas))

def tower_forward(base_rows, weight_v, weight_u, bias_c, weight_p, bias_p):
    low_rank = jnp.dot(base_rows, weight_v, preferred_element_type=jnp.float32).astype(jnp.bfloat16)
    crossed = jnp.dot(low_rank, weight_u, preferred_element_type=jnp.float32)
    base_f = base_rows.astype(jnp.float32)
    mixed = (base_f * (crossed + bias_c) + base_f).astype(jnp.bfloat16)
    pre_act = jnp.dot(mixed, weight_p, preferred_element_type=jnp.float32) + bias_p
    tower_out = jax.nn.silu(pre_act).astype(jnp.bfloat16)
    return (low_rank, crossed, mixed, pre_act, tower_out)

def tower_backward(base_rows, weight_v, weight_u, bias_c, weight_p, bias_p, grad_out):
    low_rank, crossed, mixed, pre_act, tower_out = tower_forward(base_rows, weight_v, weight_u, bias_c, weight_p, bias_p)
    grad_pre = grad_out.astype(jnp.float32) * silu_grad(pre_act)
    grad_pbias = lax.optimization_barrier(jnp.sum(grad_pre, axis=0))
    grad_pre_b = grad_pre.astype(jnp.bfloat16)
    grad_pw = inner_rows(mixed, grad_pre_b)
    grad_mixed = outer_cols(grad_pre_b, weight_p)
    base_f = base_rows.astype(jnp.float32)
    grad_cross = grad_mixed * base_f
    grad_cbias = lax.optimization_barrier(jnp.sum(grad_cross, axis=0))
    grad_cross_b = grad_cross.astype(jnp.bfloat16)
    grad_uw = inner_rows(low_rank, grad_cross_b)
    grad_low = outer_cols(grad_cross_b, weight_u).astype(jnp.bfloat16)
    grad_vw = inner_rows(base_rows, grad_low)
    grad_base = (grad_mixed * (crossed + bias_c + 1.0) + outer_cols(grad_low, weight_v)).astype(jnp.bfloat16)
    return (grad_base, grad_vw, grad_uw, grad_cbias, grad_pw, grad_pbias)

def reference(embeddings, tower_v, tower_u, cross_bias, proj_w, proj_bias, arch_v, arch_u, arch_bias, logit_w, labels):
    samples = embeddings.shape[0]
    towers = tower_v.shape[0]
    width = tower_v.shape[1]
    stacked = jnp.transpose(embeddings.reshape(samples, towers, width), (1, 0, 2))

    def forward_one(operands):
        base_rows, weight_v, weight_u, bias_c, weight_p, bias_p = operands
        return tower_forward(base_rows, weight_v, weight_u, bias_c, weight_p, bias_p)[4]
    outputs = lax.map(forward_one, (stacked, tower_v, tower_u, cross_bias, proj_w, proj_bias))
    proj_width = outputs.shape[2]
    arch_in = jnp.transpose(outputs, (1, 0, 2)).reshape(samples, towers * proj_width)
    arch_low = jnp.dot(arch_in, arch_v, preferred_element_type=jnp.float32).astype(jnp.bfloat16)
    arch_cross = jnp.dot(arch_low, arch_u, preferred_element_type=jnp.float32)
    arch_f = arch_in.astype(jnp.float32)
    arch_mix = (arch_f * (arch_cross + arch_bias) + arch_f).astype(jnp.bfloat16)
    mix_f = arch_mix.astype(jnp.float32)
    logits = lax.optimization_barrier(jnp.sum(mix_f * logit_w, axis=1))
    grad_logits = (jax.nn.sigmoid(logits) - labels) * (LOSS_SCALE / TOKENS)
    grad_logit_w = lax.optimization_barrier(jnp.sum(grad_logits[:, None] * mix_f, axis=0))
    grad_mix = grad_logits[:, None] * logit_w[None, :]
    grad_arch_cross = grad_mix * arch_f
    grad_arch_bias = lax.optimization_barrier(jnp.sum(grad_arch_cross, axis=0))
    grad_arch_cross_b = grad_arch_cross.astype(jnp.bfloat16)
    grad_arch_u = inner_rows(arch_low, grad_arch_cross_b)
    grad_arch_low = outer_cols(grad_arch_cross_b, arch_u).astype(jnp.bfloat16)
    grad_arch_v = inner_rows(arch_in, grad_arch_low)
    grad_arch_in = (grad_mix * (arch_cross + arch_bias + 1.0) + outer_cols(grad_arch_low, arch_v)).astype(jnp.bfloat16)
    grad_outs = jnp.transpose(grad_arch_in.reshape(samples, towers, proj_width), (1, 0, 2))

    def backward_one(operands):
        base_rows, weight_v, weight_u, bias_c, weight_p, bias_p, grad_out = operands
        return tower_backward(base_rows, weight_v, weight_u, bias_c, weight_p, bias_p, grad_out)
    grad_base, grad_vw, grad_uw, grad_cbias, grad_pw, grad_pbias = lax.map(backward_one, (stacked, tower_v, tower_u, cross_bias, proj_w, proj_bias, grad_outs))
    emb_grad = jnp.transpose(grad_base, (1, 0, 2)).reshape(samples, towers * width)
    return (emb_grad, grad_vw, grad_uw, grad_cbias, grad_pw, grad_pbias, grad_arch_v, grad_arch_u, grad_arch_bias, grad_logit_w)
```

```python
import functools

import jax
import jax.numpy as jnp
from jax import lax
from jax.experimental import pallas as pl
from jax.experimental.pallas import tpu as pltpu
from jax.sharding import PartitionSpec as P

LOSS_SCALE = 1024
NC = 2
F32 = jnp.float32
BF16 = jnp.bfloat16
MESH = pl.DeviceIdType.MESH


def dot(a, b):
    return jnp.dot(a, b, preferred_element_type=F32)


def dot_t(a, b):
    return lax.dot_general(a, b, (((1,), (1,)), ((), ())), preferred_element_type=F32)


def kernel(
    dims,
    emb, tv_h, tu_h, cb, pw_h, pb, av_h, au_h, ab, lw, labels,
    emb_out, vw_out, uw_out, cb_out, pw_out, pb_out, gav_out, gau_out, gab_out, glw_out,
    base, tv, tu, pw, av, au,
    low, scale, mixed, sgrad, gpre, gcb, glow,
    out, arch_in, back_s, back_r, ag, eg,
    vw_acc, uw_acc, pw_acc, cb_acc, pb_acc, vec_acc,
    w_s, w_r, u_s, u_r, a1_s, a1_r, a2_s, a2_r,
    local_sem, fwd_ss, fwd_rs, out_ss, out_rs, back_ss, back_rs, ag_ss, ag_rs,
    emb_ss, emb_rs, w_ss, w_rs, u_ss, u_rs, a1_ss, a1_rs, a2_ss, a2_rs,
):
    T, D, SB, OC = dims["T"], dims["D"], dims["SB"], dims["OC"]
    HI = 2
    DY = D // HI
    SC = SB // NC
    R = T * SC
    W = D * OC
    RANK, PROJ, AR = dims["RANK"], dims["PROJ"], dims["AR"]
    ARCH = T * PROJ
    RR = RANK // D
    AP = PROJ // D
    UR = AR // T
    UF = UR // D
    t = lax.axis_index("tower")
    d = lax.axis_index("dev")
    d_hi = lax.div(d, DY)
    d_y = lax.rem(d, DY)

    def dev(k):
        hi = lax.rem(d_hi + lax.div(k, DY), HI)
        return hi * DY + lax.rem(d_y + lax.rem(k, DY), DY)

    def tow(k):
        return lax.rem(t + k, T)

    def cols(j, n):
        return pl.ds(pl.multiple_of(j * n, n), n)

    def loop(lo, hi, f):
        lax.fori_loop(lo, hi, lambda i, x: (f(i), x)[1], 0)

    def remote(src, dst, ss, rs, who):
        return pltpu.make_async_remote_copy(
            src_ref=src, dst_ref=dst, send_sem=ss, recv_sem=rs, device_id=who, device_id_type=MESH
        )

    barrier = pltpu.get_barrier_semaphore()
    loop(1, D, lambda k: pl.semaphore_signal(
        barrier, inc=1, device_id=(t, dev(jnp.int32(k))), device_id_type=MESH))
    loop(1, T, lambda k: pl.semaphore_signal(
        barrier, inc=1, device_id=(tow(k), d), device_id_type=MESH))
    pl.semaphore_wait(barrier, D + T - 2)

    def fwd(c, k):
        j = dev(k)
        return remote(
            emb.at[:, j, pl.ds(c * SC, SC), :], base.at[c, :, :, cols(d, OC)],
            fwd_ss.at[c, k], fwd_rs.at[c, d], (t, j))

    def fwd_arrival(c, k):
        j = dev(k)
        return remote(
            emb.at[:, j, pl.ds(c * SC, SC), :], base.at[c, :, :, cols(j, OC)],
            fwd_ss.at[c, k], fwd_rs.at[c, j], (t, j))

    def tower_out(c, k):
        j = tow(k)
        return remote(
            out.at[c, j], arch_in.at[c, :, cols(t, PROJ)],
            out_ss.at[c, k], out_rs.at[c, t], (j, d))

    def tower_out_arrival(c, k):
        j = tow(k)
        return remote(
            out.at[c, j], arch_in.at[c, :, cols(j, PROJ)],
            out_ss.at[c, k], out_rs.at[c, j], (j, d))

    def back(c, k, who):
        j = tow(k)
        return remote(
            back_s.at[c, j], back_r.at[c, who], back_ss.at[c, k], back_rs.at[c, who], (j, d))

    def gather(c, k, who):
        j = tow(k)
        return remote(ag.at[c, t], ag.at[c, who], ag_ss.at[c, k], ag_rs.at[c, who], (j, d))

    def emb_back(c, k, who):
        j = dev(k)
        return remote(
            eg.at[c, j], emb_out.at[:, who, pl.ds(c * SC, SC), :],
            emb_ss.at[c, k], emb_rs.at[c, who], (t, j))

    def over_dev(s, r, ss, rs):
        def make(k, who):
            j = dev(k)
            return remote(s.at[j], r.at[who], ss.at[k], rs.at[who], (t, j))
        return make

    w_copy = over_dev(w_s, w_r, w_ss, w_rs)
    u_copy = over_dev(u_s, u_r, u_ss, u_rs)
    a2_copy = over_dev(a2_s, a2_r, a2_ss, a2_rs)

    def a1_copy(k, who):
        j = tow(k)
        return remote(a1_s.at[j], a1_r.at[who], a1_ss.at[k], a1_rs.at[who], (j, d))

    def fwd_own(c):
        return pltpu.make_async_copy(
            emb.at[:, d, pl.ds(c * SC, SC), :], base.at[c, :, :, cols(d, OC)], local_sem.at[c])

    def emb_own(c):
        return pltpu.make_async_copy(
            eg.at[c, d], emb_out.at[:, d, pl.ds(c * SC, SC), :], local_sem.at[NC + c])

    weights = [
        pltpu.make_async_copy(src, dst, local_sem.at[2 * NC + i])
        for i, (src, dst) in enumerate(
            [(tv_h, tv), (tu_h, tu), (pw_h, pw), (av_h, av), (au_h, au)])
    ]

    def start_fwd(c):
        loop(1, D, lambda k: fwd(c, k).start())

    for c in range(NC):
        start_fwd(c)
    for w in weights:
        w.start()
    for c in range(NC):
        fwd_own(c).start()

    vw_acc[...] = jnp.zeros_like(vw_acc)
    uw_acc[...] = jnp.zeros_like(uw_acc)
    pw_acc[...] = jnp.zeros_like(pw_acc)
    cb_acc[...] = jnp.zeros_like(cb_acc)
    pb_acc[...] = jnp.zeros_like(pb_acc)
    vec_acc[...] = jnp.zeros_like(vec_acc)
    for w in weights:
        w.wait()

    def chunk(c):
        fwd_own(c).wait()
        loop(1, D, lambda k: fwd_arrival(c, k).wait_recv())
        low[...] = dot(base[c].reshape(R, W), tv[...]).astype(BF16)

        def forward_cols(j):
            at = cols(j, OC)
            s = dot(low[...], tu[:, at]) + (cb[:, at] + 1.0)
            scale[:, at] = s
            b = base[c, :, :, at].reshape(R, OC).astype(F32)
            mixed[:, at] = (b * s).astype(BF16)

        loop(0, D, forward_cols)
        pre = dot(mixed[...], pw[...]) + pb[...]
        sig = jax.nn.sigmoid(pre)
        sgrad[...] = sig * (1.0 + pre * (1.0 - sig))
        out[c] = (pre * sig).astype(BF16).reshape(T, SC, PROJ)
        loop(1, T, lambda k: tower_out(c, k).start())
        arch_in[c, :, cols(t, PROJ)] = out[c, t]
        loop(1, T, lambda k: tower_out_arrival(c, k).wait_recv())

        a_in = arch_in[c]
        a_low = dot(a_in, av[...]).astype(BF16)
        a_scale = dot(a_low, au[...]) + (ab[...] + 1.0)
        a_f = a_in.astype(F32)
        mix = (a_f * a_scale).astype(BF16).astype(F32)
        logits = jnp.sum(mix * lw[...], axis=1, keepdims=True)
        row = lax.broadcasted_iota(jnp.int32, (SC, SB), 0) + c * SC
        lane = lax.broadcasted_iota(jnp.int32, (SC, SB), 1)
        label = jnp.sum(
            jnp.where(row == lane, jnp.broadcast_to(labels[...], (SC, SB)), 0.0),
            axis=1, keepdims=True)
        g = (jax.nn.sigmoid(logits) - label) * (LOSS_SCALE / (T * D * SB))
        vec_acc[1:2, :] += jnp.sum(g * mix, axis=0, keepdims=True)
        g_mix = g * lw[...]
        g_cross = g_mix * a_f
        vec_acc[0:1, :] += jnp.sum(g_cross, axis=0, keepdims=True)
        g_cross_b = g_cross.astype(BF16)
        g_low = dot_t(g_cross_b, au[...]).astype(BF16)
        g_in = (g_mix * a_scale + dot_t(g_low, av[...])).astype(BF16)
        for j in range(T):
            back_s[c, j, :, 0:PROJ] = g_in[:, j * PROJ:(j + 1) * PROJ]
            back_s[c, j, :, PROJ:2 * PROJ] = g_cross_b[:, j * PROJ:(j + 1) * PROJ]
        loop(1, T, lambda k: back(c, k, t).start())
        back_r[c, t] = back_s[c, t]
        ag[c, t, :, 0:AR] = a_low
        ag[c, t, :, AR:2 * AR] = g_low
        loop(1, T, lambda k: gather(c, k, t).start())

        loop(1, T, lambda k: back(c, k, tow(k)).wait_recv())
        g_pre = back_r[c, :, :, 0:PROJ].reshape(R, PROJ).astype(F32) * sgrad[...]
        pb_acc[...] += jnp.sum(g_pre, axis=0, keepdims=True)
        gpre[...] = g_pre.astype(BF16)

        def backward_cols(j):
            at = cols(j, OC)
            gm = dot_t(gpre[...], pw[at, :])
            gc = gm * base[c, :, :, at].reshape(R, OC).astype(F32)
            cb_acc[:, at] += jnp.sum(gc, axis=0, keepdims=True)
            gcb[:, at] = gc.astype(BF16)
            scale[:, at] = gm * scale[:, at]

        loop(0, D, backward_cols)
        glow[...] = dot_t(gcb[...], tu[...]).astype(BF16)

        def grad_cols(j):
            at = cols(j, OC)
            v = scale[:, at] + dot_t(glow[...], tv[at, :])
            eg[c, j] = v.astype(BF16).reshape(T, SC, OC)

        def grad_send(k):
            grad_cols(dev(k))
            emb_back(c, k, d).start()

        loop(1, D, grad_send)
        grad_cols(d)
        emb_own(c).start()

        glow_t = glow[...].T
        low_t = low[...].T
        gpre_t = gpre[...].T

        def weight_cols(j):
            at = cols(j, OC)
            vw_acc[:, at] += dot(glow_t, base[c, :, :, at].reshape(R, OC))
            uw_acc[:, at] += dot(low_t, gcb[:, at])
            pw_acc[:, at] += dot(gpre_t, mixed[:, at])

        loop(0, D, weight_cols)

    loop(0, NC, chunk)

    for c in range(NC):
        loop(1, T, lambda k: gather(c, k, tow(k)).wait_recv())
    gathered = ag[...].reshape(NC * R, 2 * AR)
    gav = dot(out[...].reshape(NC * R, PROJ).T, gathered[:, AR:])
    gau = dot(back_r[:, :, :, PROJ:].reshape(NC * R, PROJ).T, gathered[:, :AR]).T
    for j in range(T):
        a1_s[j, 0:UR, :] = gau[j * UR:(j + 1) * UR, :]
        a1_s[j, UR:UR + 8, :] = vec_acc[:, j * PROJ:(j + 1) * PROJ]
    loop(1, T, lambda k: a1_copy(k, t).start())
    a1_r[t] = a1_s[t]
    half = ARCH // 2
    for j in range(D):
        a2_s[j, 8:16, 0:AR] = gav[j * AP:j * AP + 8, :]
        a2_s[j, 8:16, AR:2 * AR] = gav[j * AP + 8:j * AP + 16, :]

    for j in range(D):
        at = slice(j * OC, (j + 1) * OC)
        u_s[j] = uw_acc[j * RR:(j + 1) * RR, :].astype(BF16)
        w_s[j, 0:RANK, :] = vw_acc[:, at].astype(BF16)
        w_s[j, RANK:RANK + PROJ, :] = pw_acc[:, at].astype(BF16)
        first = lax.broadcasted_iota(jnp.int32, (16, OC), 0) == 0
        pb2 = jnp.concatenate([pb_acc[...]] * (OC // PROJ), axis=1)
        w_s[j, RANK + PROJ:RANK + PROJ + 16, :] = jnp.where(
            first, jnp.broadcast_to(cb_acc[:, at], (16, OC)), jnp.broadcast_to(pb2, (16, OC))
        ).astype(BF16)

    def send_weights(k):
        u_copy(k, d).start()
        w_copy(k, d).start()

    loop(1, D, send_weights)
    u_r[d] = u_s[d]
    w_r[d] = w_s[d]

    loop(1, T, lambda k: a1_copy(k, tow(k)).wait_recv())
    vec = jnp.sum(a1_r[:, UR:UR + 8, :], axis=0)
    per = half // PROJ
    for j in range(D):
        for i in range(T):
            r0 = UF * (i // per)
            c0 = (i % per) * PROJ
            a2_s[j, r0:r0 + UF, c0:c0 + PROJ] = a1_r[i, j * UF:(j + 1) * UF, :]
        a2_s[j, 0:8, half:half + PROJ] = vec
        a2_s[j, 8:16, half:half + PROJ] = vec
    loop(1, D, lambda k: a2_copy(k, d).start())
    a2_r[d] = a2_s[d]

    loop(1, D, lambda k: a2_copy(k, dev(k)).wait_recv())
    a2 = jnp.sum(a2_r[...], axis=0)
    gau_out[:, 0:half] = a2[0:UF, 0:half]
    gau_out[:, half:] = a2[UF:2 * UF, 0:half]
    gav_out[0:8, :] = a2[8:16, 0:AR]
    gav_out[8:16, :] = a2[8:16, AR:2 * AR]
    shift = lax.rem(PROJ - d * AP, PROJ)
    vec = pltpu.roll(a2[0:8, half:half + PROJ], shift, 1)
    gab_out[...] = vec[0:1, 0:AP]
    glw_out[...] = vec[1:2, 0:AP]

    loop(1, D, lambda k: u_copy(k, dev(k)).wait_recv())
    loop(1, D, lambda k: w_copy(k, dev(k)).wait_recv())
    uw_out[...] = jnp.sum(u_r[...].astype(F32), axis=0)
    ws = jnp.sum(w_r[...].astype(F32), axis=0)
    vw_out[...] = ws[0:RANK].T
    pw_out[...] = ws[RANK:RANK + PROJ].T
    cb_out[...] = ws[RANK + PROJ:RANK + PROJ + 1]
    vec = pltpu.roll(ws[RANK + PROJ + 8:RANK + PROJ + 16, 0:PROJ], shift, 1)
    pb_out[...] = vec[0:1, 0:AP]

    for c in range(NC):
        emb_own(c).wait()

        def drain_dev(k):
            fwd(c, k).wait_send()
            emb_back(c, k, d).wait_send()
            emb_back(c, k, dev(k)).wait_recv()

        def drain_tower(k):
            tower_out(c, k).wait_send()
            back(c, k, t).wait_send()
            gather(c, k, t).wait_send()

        loop(1, D, drain_dev)
        loop(1, T, drain_tower)

    def drain_last(k):
        u_copy(k, d).wait_send()
        w_copy(k, d).wait_send()
        a2_copy(k, d).wait_send()

    loop(1, D, drain_last)
    loop(1, T, lambda k: a1_copy(k, t).wait_send())


def local(
    embeddings, tower_v, tower_u, cross_bias, proj_w, proj_bias,
    arch_v, arch_u, arch_bias, logit_w, labels,
):
    T = lax.axis_size("tower")
    D = lax.axis_size("dev")
    rows, OC = embeddings.shape
    SB = rows // (T * D)
    SC = SB // NC
    R = T * SC
    W = D * OC
    RANK = tower_v.shape[2]
    PROJ = proj_w.shape[2]
    ARCH, AR = arch_v.shape
    UR = AR // T
    AP = PROJ // D
    WR = RANK + PROJ + 16
    A2 = ARCH // 2 + PROJ
    dims = dict(T=T, D=D, SB=SB, OC=OC, RANK=RANK, PROJ=PROJ, AR=AR)
    vmem = pl.BlockSpec(memory_space=pltpu.VMEM)
    hbm = pl.BlockSpec(memory_space=pl.ANY)
    dma = pltpu.SemaphoreType.DMA
    outs = pl.pallas_call(
        functools.partial(kernel, dims),
        out_shape=(
            jax.ShapeDtypeStruct((T, D, SB, OC), BF16),
            jax.ShapeDtypeStruct((W // D, RANK), F32),
            jax.ShapeDtypeStruct((RANK // D, W), F32),
            jax.ShapeDtypeStruct((1, OC), F32),
            jax.ShapeDtypeStruct((W // D, PROJ), F32),
            jax.ShapeDtypeStruct((1, AP), F32),
            jax.ShapeDtypeStruct((AP, AR), F32),
            jax.ShapeDtypeStruct((UR // D, ARCH), F32),
            jax.ShapeDtypeStruct((1, AP), F32),
            jax.ShapeDtypeStruct((1, AP), F32),
        ),
        in_specs=[hbm, hbm, hbm, vmem, hbm, vmem, hbm, hbm, vmem, vmem, vmem],
        out_specs=(hbm,) + (vmem,) * 9,
        scratch_shapes=[
            pltpu.VMEM((NC, T, SC, W), BF16),
            pltpu.VMEM((W, RANK), BF16),
            pltpu.VMEM((RANK, W), BF16),
            pltpu.VMEM((W, PROJ), BF16),
            pltpu.VMEM((ARCH, AR), BF16),
            pltpu.VMEM((AR, ARCH), BF16),
            pltpu.VMEM((R, RANK), BF16),
            pltpu.VMEM((R, W), F32),
            pltpu.VMEM((R, W), BF16),
            pltpu.VMEM((R, PROJ), F32),
            pltpu.VMEM((R, PROJ), BF16),
            pltpu.VMEM((R, W), BF16),
            pltpu.VMEM((R, RANK), BF16),
            pltpu.VMEM((NC, T, SC, PROJ), BF16),
            pltpu.VMEM((NC, SC, ARCH), BF16),
            pltpu.VMEM((NC, T, SC, 2 * PROJ), BF16),
            pltpu.VMEM((NC, T, SC, 2 * PROJ), BF16),
            pltpu.VMEM((NC, T, SC, 2 * AR), BF16),
            pltpu.VMEM((NC, D, T, SC, OC), BF16),
            pltpu.VMEM((RANK, W), F32),
            pltpu.VMEM((RANK, W), F32),
            pltpu.VMEM((PROJ, W), F32),
            pltpu.VMEM((1, W), F32),
            pltpu.VMEM((1, PROJ), F32),
            pltpu.VMEM((8, ARCH), F32),
            pltpu.VMEM((D, WR, OC), BF16),
            pltpu.VMEM((D, WR, OC), BF16),
            pltpu.VMEM((D, RANK // D, W), BF16),
            pltpu.VMEM((D, RANK // D, W), BF16),
            pltpu.VMEM((T, UR + 8, PROJ), F32),
            pltpu.VMEM((T, UR + 8, PROJ), F32),
            pltpu.VMEM((D, 16, A2), F32),
            pltpu.VMEM((D, 16, A2), F32),
            dma((2 * NC + 5,)),
            dma((NC, D)), dma((NC, D)),
            dma((NC, T)), dma((NC, T)),
            dma((NC, T)), dma((NC, T)),
            dma((NC, T)), dma((NC, T)),
            dma((NC, D)), dma((NC, D)),
            dma((D,)), dma((D,)),
            dma((D,)), dma((D,)),
            dma((T,)), dma((T,)),
            dma((D,)), dma((D,)),
        ],
        compiler_params=pltpu.CompilerParams(
            collective_id=0, has_side_effects=True, vmem_limit_bytes=60 << 20
        ),
    )(
        embeddings.reshape(T, D, SB, OC), tower_v[0], tower_u[0], cross_bias, proj_w[0], proj_bias,
        arch_v, arch_u, arch_bias[None], logit_w[None], labels[None],
    )
    eg, vw, uw, cb, pw, pb, gav, gau, gab, glw = outs
    return (
        eg.reshape(rows, OC), vw[None], uw[None], cb, pw[None], pb,
        gav, gau, gab[0], glw[0],
    )


def solution(mesh):
    return jax.shard_map(
        local,
        mesh=mesh,
        in_specs=(
            P(None, ("tower", "dev")),
            P("tower", None, None),
            P("tower", None, None),
            P("tower", None),
            P("tower", None, None),
            P("tower", None),
            P(),
            P(),
            P(),
            P(),
            P(("tower", "dev")),
        ),
        out_specs=(
            P(None, ("tower", "dev")),
            P("tower", "dev", None),
            P("tower", "dev", None),
            P("tower", "dev"),
            P("tower", "dev", None),
            P("tower", "dev"),
            P(("tower", "dev"), None),
            P(("tower", "dev"), None),
            P(("tower", "dev")),
            P(("tower", "dev")),
        ),
        check_vma=False,
    )
```

```python
import functools

import jax
import jax.numpy as jnp
from jax import lax
from jax.experimental import pallas as pl
from jax.experimental.pallas import tpu as pltpu
from jax.sharding import PartitionSpec as P

LOSS_SCALE = 1024
NC = 4
F32 = jnp.float32
BF16 = jnp.bfloat16
MESH = pl.DeviceIdType.MESH


def dot(a, b):
    return jnp.dot(a, b, preferred_element_type=F32)


def dot_t(a, b):
    return lax.dot_general(a, b, (((1,), (1,)), ((), ())), preferred_element_type=F32)


def kernel(
    dims,
    emb, tv_h, tu_h, cb, pw_h, pb, av_h, au_h, ab, lw, labels,
    emb_land, vw_out, uw_out, cb_out, pw_out, pb_out, gav_out, gau_out, gab_out, glw_out,
    base, tv, tu, pw, av, au,
    low, scale, mixed, sgrad, gpre, gcb, glow,
    out, arch_in, back_s, back_r, ag, eg,
    cb_acc, pb_acc, vec_acc,
    w_s, w_r, u_s, u_r, a1_s, a1_r, a2_f, a2_s, a2_r,
    local_sem, fwd_ss, fwd_rs, out_ss, out_rs, back_ss, back_rs,
    agx_ss, agx_rs, agz_ss, agz_rs, agc_ss, agc_rs,
    emb_ss, emb_rs, w_ss, w_rs, u_ss, u_rs, a1_ss, a1_rs, a2_ss, a2_rs,
):
    T, D, SB, OC = dims["T"], dims["D"], dims["SB"], dims["OC"]
    HI = 2
    DY = D // HI
    SC = SB // NC
    R = T * SC
    W = D * OC
    RANK, PROJ, AR = dims["RANK"], dims["PROJ"], dims["AR"]
    ARCH = T * PROJ
    RR = RANK // D
    AP = PROJ // D
    UR = AR // T
    UF = UR // D
    t = lax.axis_index("tower")
    d = lax.axis_index("dev")
    d_hi = lax.div(d, DY)
    d_y = lax.rem(d, DY)
    t_zx = lax.div(t, 2)
    t_core = lax.rem(t, 2)
    t_z = lax.div(t, 4)
    t_zx_beside = 2 * t_z + 1 - lax.rem(t_zx, 2)

    def dev(k):
        hi = lax.rem(d_hi + lax.div(k, DY), HI)
        return hi * DY + lax.rem(d_y + lax.rem(k, DY), DY)

    def tow(k):
        return lax.rem(t + k, T)

    def cols(j, n):
        return pl.ds(pl.multiple_of(j * n, n), n)

    def loop(lo, hi, f):
        lax.fori_loop(lo, hi, lambda i, x: (f(i), x)[1], 0)

    def remote(src, dst, ss, rs, who):
        return pltpu.make_async_remote_copy(
            src_ref=src, dst_ref=dst, send_sem=ss, recv_sem=rs, device_id=who, device_id_type=MESH
        )

    barrier = pltpu.get_barrier_semaphore()
    loop(1, D, lambda k: pl.semaphore_signal(
        barrier, inc=1, device_id=(t, dev(jnp.int32(k))), device_id_type=MESH))
    loop(1, T, lambda k: pl.semaphore_signal(
        barrier, inc=1, device_id=(tow(k), d), device_id_type=MESH))
    pl.semaphore_wait(barrier, D + T - 2)

    def fwd(c, k):
        j = dev(k)
        return remote(
            emb.at[:, j, pl.ds(c * SC, SC), :], base.at[c, :, :, cols(d, OC)],
            fwd_ss.at[c, k], fwd_rs.at[c, d], (t, j))

    def fwd_arrival(c, k):
        j = dev(k)
        return remote(
            emb.at[:, j, pl.ds(c * SC, SC), :], base.at[c, :, :, cols(j, OC)],
            fwd_ss.at[c, k], fwd_rs.at[c, j], (t, j))

    def tower_out(c, k):
        j = tow(k)
        return remote(
            out.at[c, j], arch_in.at[c, :, cols(t, PROJ)],
            out_ss.at[c, k], out_rs.at[c, t], (j, d))

    def tower_out_arrival(c, k):
        j = tow(k)
        return remote(
            out.at[c, j], arch_in.at[c, :, cols(j, PROJ)],
            out_ss.at[c, k], out_rs.at[c, j], (j, d))

    def back(c, k, who):
        j = tow(k)
        return remote(
            back_s.at[c, j], back_r.at[c, who], back_ss.at[c, k], back_rs.at[c, who], (j, d))

    def pair(c, z, core):
        return ag.at[c, pl.ds(2 * z, 2), core]

    def gather_x(c, own):
        zx = t_zx if own else t_zx_beside
        src = ag.at[c, t_zx, t_core]
        return remote(
            src, ag.at[c, zx, t_core], agx_ss.at[c], agx_rs.at[c],
            (2 * t_zx_beside + t_core, d))

    def gather_z(c, k, own):
        z = lax.rem(t_z + k, T // 4)
        who = t_z if own else z
        return remote(
            pair(c, t_z, t_core), pair(c, who, t_core), agz_ss.at[c, k], agz_rs.at[c, who],
            (4 * z + lax.rem(t, 4), d))

    def gather_core(c, own):
        core = t_core if own else 1 - t_core
        return remote(
            ag.at[c, :, t_core], ag.at[c, :, core], agc_ss.at[c], agc_rs.at[c],
            (2 * t_zx + 1 - t_core, d))

    def emb_back(c, k, who):
        j = dev(k)
        return remote(
            eg.at[c, j], emb_land.at[:, who, pl.ds(c * SC, SC), :],
            emb_ss.at[c, k], emb_rs.at[c, who], (t, j))

    def over_dev(s, r, ss, rs):
        def make(k, who):
            j = dev(k)
            return remote(s.at[j], r.at[who], ss.at[k], rs.at[who], (t, j))
        return make

    w_copy = over_dev(w_s, w_r, w_ss, w_rs)
    u_copy = over_dev(u_s, u_r, u_ss, u_rs)
    a2_copy = over_dev(a2_s, a2_r, a2_ss, a2_rs)

    def a1_copy(k, who):
        j = tow(k)
        return remote(a1_s.at[j], a1_r.at[who], a1_ss.at[k], a1_rs.at[who], (j, d))

    def fwd_own(c):
        return pltpu.make_async_copy(
            emb.at[:, d, pl.ds(c * SC, SC), :], base.at[c, :, :, cols(d, OC)], local_sem.at[c])

    def emb_own(c):
        return pltpu.make_async_copy(
            eg.at[c, d], emb_land.at[:, d, pl.ds(c * SC, SC), :], local_sem.at[NC + c])

    weights = [
        pltpu.make_async_copy(src, dst, local_sem.at[2 * NC + i])
        for i, (src, dst) in enumerate(
            [(tv_h, tv), (tu_h, tu), (pw_h, pw), (av_h, av), (au_h, au)])
    ]

    def start_fwd(c):
        loop(1, D, lambda k: fwd(c, k).start())

    for c in range(2):
        start_fwd(c)
    for w in weights:
        w.start()
    for c in range(NC):
        fwd_own(c).start()

    cb_acc[...] = jnp.zeros_like(cb_acc)
    pb_acc[...] = jnp.zeros_like(pb_acc)
    vec_acc[...] = jnp.zeros_like(vec_acc)
    for w in weights:
        w.wait()

    def forward(c):
        slot = lax.rem(c, 3)
        fwd_own(c).wait()
        loop(1, D, lambda k: fwd_arrival(c, k).wait_recv())
        low[c] = dot(base[c].reshape(R, W), tv[...]).astype(BF16)

        def forward_cols(j):
            at = cols(j, OC)
            s = dot(low[c], tu[:, at]) + (cb[:, at] + 1.0)
            scale[slot, :, at] = s
            b = base[c, :, :, at].reshape(R, OC).astype(F32)
            mixed[c, :, at] = (b * s).astype(BF16)

        loop(0, D, forward_cols)
        pre = dot(mixed[c], pw[...]) + pb[...]
        sig = jax.nn.sigmoid(pre)
        sgrad[slot] = sig * (1.0 + pre * (1.0 - sig))
        out[c] = (pre * sig).astype(BF16).reshape(T, SC, PROJ)
        loop(1, T, lambda k: tower_out(c, k).start())
        arch_in[c, :, cols(t, PROJ)] = out[c, t]

        @pl.when(c + 2 < NC)
        def _():
            start_fwd(c + 2)

    def over_arch(c):
        loop(1, T, lambda k: tower_out_arrival(c, k).wait_recv())
        a_in = arch_in[c]
        a_low = dot(a_in, av[...]).astype(BF16)
        a_scale = dot(a_low, au[...]) + (ab[...] + 1.0)
        a_f = a_in.astype(F32)
        mix = (a_f * a_scale).astype(BF16).astype(F32)
        logits = jnp.sum(mix * lw[...], axis=1, keepdims=True)
        row = lax.broadcasted_iota(jnp.int32, (SC, SB), 0) + c * SC
        lane = lax.broadcasted_iota(jnp.int32, (SC, SB), 1)
        label = jnp.sum(
            jnp.where(row == lane, jnp.broadcast_to(labels[...], (SC, SB)), 0.0),
            axis=1, keepdims=True)
        g = (jax.nn.sigmoid(logits) - label) * (LOSS_SCALE / (T * D * SB))
        g_mix = g * lw[...]
        g_cross = g_mix * a_f
        g_low = dot_t(g_cross.astype(BF16), au[...]).astype(BF16)
        g_in = (g_mix * a_scale + dot_t(g_low, av[...])).astype(BF16)
        for j in range(T):
            back_s[c, j] = g_in[:, j * PROJ:(j + 1) * PROJ]
        loop(1, T, lambda k: back(c, k, t).start())
        back_r[c, t] = back_s[c, t]
        ag[c, t_zx, t_core, :, 0:AR] = a_low
        ag[c, t_zx, t_core, :, AR:2 * AR] = g_low
        g_wide = jnp.broadcast_to(g, (SC, PROJ))
        g_high = g_wide.astype(BF16)
        ag[c, t_zx, t_core, :, 2 * AR:2 * AR + PROJ] = g_high
        ag[c, t_zx, t_core, :, 2 * AR + PROJ:] = (g_wide - g_high.astype(F32)).astype(BF16)
        gather_x(c, True).start()
        vec_acc[0:1, :] += jnp.sum(g_cross, axis=0, keepdims=True)
        vec_acc[1:2, :] += jnp.sum(g * mix, axis=0, keepdims=True)

    def backward(c):
        slot = lax.rem(c, 3)
        loop(1, T, lambda k: back(c, k, tow(k)).wait_recv())
        gather_x(c, False).wait_recv()
        loop(1, T // 4, lambda k: gather_z(c, k, True).start())
        g_pre = back_r[c].reshape(R, PROJ).astype(F32) * sgrad[slot]
        pb_acc[...] += jnp.sum(g_pre, axis=0, keepdims=True)
        gpre[c] = g_pre.astype(BF16)

        def backward_cols(j):
            at = cols(j, OC)
            gm = dot_t(gpre[c], pw[at, :])
            gc = gm * base[c, :, :, at].reshape(R, OC).astype(F32)
            cb_acc[:, at] += jnp.sum(gc, axis=0, keepdims=True)
            gcb[c, :, at] = gc.astype(BF16)
            scale[slot, :, at] = gm * scale[slot, :, at]

        loop(0, D, backward_cols)
        glow[c] = dot_t(gcb[c], tu[...]).astype(BF16)

        def grad_cols(j):
            at = cols(j, OC)
            v = scale[slot, :, at] + dot_t(glow[c], tv[at, :])
            eg[c, j] = v.astype(BF16).reshape(T, SC, OC)

        def grad_send(k):
            grad_cols(dev(k))
            emb_back(c, k, d).start()

        loop(1, D, grad_send)
        grad_cols(d)
        emb_own(c).start()

        @pl.when(c > 0)
        def _():
            gather_last(c - 1)

    def gather_last(c):
        loop(1, T // 4, lambda k: gather_z(c, k, False).wait_recv())
        gather_core(c, True).start()

    def step(i):
        @pl.when(i < NC)
        def _():
            forward(i)

        @pl.when(jnp.logical_and(i >= 1, i <= NC))
        def _():
            over_arch(i - 1)

        @pl.when(i >= 2)
        def _():
            backward(i - 2)

    loop(0, NC + 2, step)

    N = NC * R
    low_t = low[...].reshape(N, RANK).T

    def u_cols(j):
        at = cols(j, OC)
        v = dot(low_t, gcb[:, :, at].reshape(N, OC))
        u_s[:, :, at] = v.astype(BF16).reshape(D, RR, OC)

    loop(0, D, u_cols)
    loop(1, D, lambda k: u_copy(k, d).start())
    u_r[d] = u_s[d]
    gather_last(NC - 1)
    glow_t = glow[...].reshape(N, RANK).T
    gpre_t = gpre[...].reshape(N, PROJ).T
    first = lax.broadcasted_iota(jnp.int32, (16, OC), 0) == 0
    pb2 = jnp.broadcast_to(jnp.concatenate([pb_acc[...]] * (OC // PROJ), axis=1), (16, OC))

    def w_cols(j):
        at = cols(j, OC)
        w_s[j, 0:RANK, :] = dot(glow_t, base[:, :, :, at].reshape(N, OC)).astype(BF16)
        w_s[j, RANK:RANK + PROJ, :] = dot(gpre_t, mixed[:, :, at].reshape(N, OC)).astype(BF16)
        w_s[j, RANK + PROJ:RANK + PROJ + 16, :] = jnp.where(
            first, jnp.broadcast_to(cb_acc[:, at], (16, OC)), pb2).astype(BF16)

    loop(0, D, w_cols)

    loop(0, NC, lambda c: gather_core(c, False).wait_recv())
    outs = out[...].reshape(N, PROJ)
    factors = ag[...].reshape(N, 2 * AR + 2 * PROJ)
    g = factors[:, 2 * AR:2 * AR + PROJ].astype(F32) + factors[:, 2 * AR + PROJ:].astype(F32)
    g_cross_t = (g * lw[:, cols(t, PROJ)] * outs.astype(F32)).astype(BF16).T
    gau = dot(g_cross_t, factors[:, :AR]).T
    zeros = jnp.zeros((8, PROJ), F32)
    for j in range(T):
        a1_s[j, 0:UR, :] = gau[j * UR:(j + 1) * UR, :].astype(BF16)
        a1_s[j, UR:UR + 16, :] = jnp.concatenate(
            [vec_acc[:, j * PROJ:(j + 1) * PROJ], zeros], axis=0).astype(BF16)
    loop(1, T, lambda k: a1_copy(k, t).start())
    a1_r[t] = a1_s[t]

    loop(1, D, lambda k: w_copy(k, d).start())
    w_r[d] = w_s[d]

    gav = dot(outs.T, factors[:, AR:2 * AR])
    half = ARCH // 2
    for j in range(D):
        a2_f[j, 8:16, 0:AR] = gav[j * AP:j * AP + 8, :]
        a2_f[j, 8:16, AR:2 * AR] = gav[j * AP + 8:j * AP + 16, :]
    loop(1, T, lambda k: a1_copy(k, tow(k)).wait_recv())
    vec = jnp.sum(a1_r[:, UR:UR + 16, :].astype(F32), axis=0)
    per = half // PROJ
    for i in range(T):
        part = a1_r[i, 0:UR, :].astype(F32)
        r0 = UF * (i // per)
        c0 = (i % per) * PROJ
        for j in range(D):
            a2_f[j, r0:r0 + UF, c0:c0 + PROJ] = part[j * UF:(j + 1) * UF, :]
    for j in range(D):
        a2_f[j, :, half:half + PROJ] = vec
    a2_s[...] = a2_f[...].astype(BF16)
    loop(1, D, lambda k: a2_copy(k, d).start())
    a2_r[d] = a2_s[d]

    loop(1, D, lambda k: u_copy(k, dev(k)).wait_recv())
    loop(1, D, lambda k: w_copy(k, dev(k)).wait_recv())
    uw_out[...] = jnp.sum(u_r[...].astype(F32), axis=0)
    ws = jnp.sum(w_r[...].astype(F32), axis=0)
    vw_out[...] = ws[0:RANK].T
    pw_out[...] = ws[RANK:RANK + PROJ].T
    cb_out[...] = ws[RANK + PROJ:RANK + PROJ + 1]
    shift = lax.rem(PROJ - d * AP, PROJ)
    vec = pltpu.roll(ws[RANK + PROJ + 8:RANK + PROJ + 16, 0:PROJ], shift, 1)
    pb_out[...] = vec[0:1, 0:AP]

    loop(1, D, lambda k: a2_copy(k, dev(k)).wait_recv())
    a2 = jnp.sum(a2_r[...].astype(F32), axis=0)
    gau_out[:, 0:half] = a2[0:UF, 0:half]
    gau_out[:, half:] = a2[UF:2 * UF, 0:half]
    gav_out[0:8, :] = a2[8:16, 0:AR]
    gav_out[8:16, :] = a2[8:16, AR:2 * AR]
    vec = pltpu.roll(a2[0:8, half:half + PROJ], shift, 1)
    gab_out[...] = vec[0:1, 0:AP]
    glw_out[...] = vec[1:2, 0:AP]

    for c in range(NC):
        emb_own(c).wait()

        def drain_dev(k):
            fwd(c, k).wait_send()
            emb_back(c, k, d).wait_send()
            emb_back(c, k, dev(k)).wait_recv()

        def drain_tower(k):
            tower_out(c, k).wait_send()
            back(c, k, t).wait_send()

        gather_x(c, True).wait_send()
        gather_core(c, True).wait_send()
        loop(1, T // 4, lambda k: gather_z(c, k, True).wait_send())
        loop(1, D, drain_dev)
        loop(1, T, drain_tower)

    def drain_last(k):
        u_copy(k, d).wait_send()
        w_copy(k, d).wait_send()
        a2_copy(k, d).wait_send()

    loop(1, D, drain_last)
    loop(1, T, lambda k: a1_copy(k, t).wait_send())


def deliver(*refs):
    n = (len(refs) - 1) // 2
    src, dst, sem = refs[:n], refs[n:-1], refs[-1]
    copies = [
        pltpu.make_async_copy(src[0].at[i], dst[0].at[i], sem.at[i]) for i in range(src[0].shape[0])
    ]
    for copy in copies:
        copy.start()
    for a, b in zip(src[1:], dst[1:]):
        b[...] = a[...]
    for copy in copies:
        copy.wait()


def local(
    embeddings, tower_v, tower_u, cross_bias, proj_w, proj_bias,
    arch_v, arch_u, arch_bias, logit_w, labels,
):
    T = lax.axis_size("tower")
    D = lax.axis_size("dev")
    rows, OC = embeddings.shape
    SB = rows // (T * D)
    SC = SB // NC
    R = T * SC
    W = D * OC
    RANK = tower_v.shape[2]
    PROJ = proj_w.shape[2]
    ARCH, AR = arch_v.shape
    UR = AR // T
    AP = PROJ // D
    WR = RANK + PROJ + 16
    AGW = 2 * AR + 2 * PROJ
    A2 = ARCH // 2 + PROJ
    dims = dict(T=T, D=D, SB=SB, OC=OC, RANK=RANK, PROJ=PROJ, AR=AR)
    vmem = pl.BlockSpec(memory_space=pltpu.VMEM)
    hbm = pl.BlockSpec(memory_space=pl.ANY)
    dma = pltpu.SemaphoreType.DMA
    outs = pl.pallas_call(
        functools.partial(kernel, dims),
        out_shape=(
            jax.ShapeDtypeStruct((T, D, SB, OC), BF16),
            jax.ShapeDtypeStruct((W // D, RANK), F32),
            jax.ShapeDtypeStruct((RANK // D, W), F32),
            jax.ShapeDtypeStruct((1, OC), F32),
            jax.ShapeDtypeStruct((W // D, PROJ), F32),
            jax.ShapeDtypeStruct((1, AP), F32),
            jax.ShapeDtypeStruct((AP, AR), F32),
            jax.ShapeDtypeStruct((UR // D, ARCH), F32),
            jax.ShapeDtypeStruct((1, AP), F32),
            jax.ShapeDtypeStruct((1, AP), F32),
        ),
        in_specs=[hbm, hbm, hbm, vmem, hbm, vmem, hbm, hbm, vmem, vmem, vmem],
        out_specs=(hbm,) + (vmem,) * 9,
        scratch_shapes=[
            pltpu.VMEM((NC, T, SC, W), BF16),
            pltpu.VMEM((W, RANK), BF16),
            pltpu.VMEM((RANK, W), BF16),
            pltpu.VMEM((W, PROJ), BF16),
            pltpu.VMEM((ARCH, AR), BF16),
            pltpu.VMEM((AR, ARCH), BF16),
            pltpu.VMEM((NC, R, RANK), BF16),
            pltpu.VMEM((3, R, W), F32),
            pltpu.VMEM((NC, R, W), BF16),
            pltpu.VMEM((3, R, PROJ), F32),
            pltpu.VMEM((NC, R, PROJ), BF16),
            pltpu.VMEM((NC, R, W), BF16),
            pltpu.VMEM((NC, R, RANK), BF16),
            pltpu.VMEM((NC, T, SC, PROJ), BF16),
            pltpu.VMEM((NC, SC, ARCH), BF16),
            pltpu.VMEM((NC, T, SC, PROJ), BF16),
            pltpu.VMEM((NC, T, SC, PROJ), BF16),
            pltpu.VMEM((NC, T // 2, 2, SC, AGW), BF16),
            pltpu.VMEM((NC, D, T, SC, OC), BF16),
            pltpu.VMEM((1, W), F32),
            pltpu.VMEM((1, PROJ), F32),
            pltpu.VMEM((8, ARCH), F32),
            pltpu.VMEM((D, WR, OC), BF16),
            pltpu.VMEM((D, WR, OC), BF16),
            pltpu.VMEM((D, RANK // D, W), BF16),
            pltpu.VMEM((D, RANK // D, W), BF16),
            pltpu.VMEM((T, UR + 16, PROJ), BF16),
            pltpu.VMEM((T, UR + 16, PROJ), BF16),
            pltpu.VMEM((D, 16, A2), F32),
            pltpu.VMEM((D, 16, A2), BF16),
            pltpu.VMEM((D, 16, A2), BF16),
            dma((2 * NC + 5,)),
            dma((NC, D)), dma((NC, D)),
            dma((NC, T)), dma((NC, T)),
            dma((NC, T)), dma((NC, T)),
            dma((NC,)), dma((NC,)),
            dma((NC, T // 4)), dma((NC, T // 4)),
            dma((NC,)), dma((NC,)),
            dma((NC, D)), dma((NC, D)),
            dma((D,)), dma((D,)),
            dma((D,)), dma((D,)),
            dma((T,)), dma((T,)),
            dma((D,)), dma((D,)),
        ],
        compiler_params=pltpu.CompilerParams(
            collective_id=0, has_side_effects=True, vmem_limit_bytes=60 << 20
        ),
    )(
        embeddings.reshape(T, D, SB, OC), tower_v[0], tower_u[0], cross_bias, proj_w[0], proj_bias,
        arch_v, arch_u, arch_bias[None], logit_w[None], labels[None],
    )
    eg, vw, uw, cb, pw, pb, gav, gau, gab, glw = pl.pallas_call(
        deliver,
        out_shape=tuple(jax.ShapeDtypeStruct(x.shape, x.dtype) for x in outs),
        in_specs=[hbm] + [vmem] * 9,
        out_specs=(hbm,) + (vmem,) * 9,
        scratch_shapes=[dma((T,))],
        compiler_params=pltpu.CompilerParams(vmem_limit_bytes=8 << 20),
    )(*outs)
    return (
        eg.reshape(rows, OC), vw[None], uw[None], cb, pw[None], pb,
        gav, gau, gab[0], glw[0],
    )


def solution(mesh):
    return jax.shard_map(
        local,
        mesh=mesh,
        in_specs=(
            P(None, ("tower", "dev")),
            P("tower", None, None),
            P("tower", None, None),
            P("tower", None),
            P("tower", None, None),
            P("tower", None),
            P(),
            P(),
            P(),
            P(),
            P(("tower", "dev")),
        ),
        out_specs=(
            P(None, ("tower", "dev")),
            P("tower", "dev", None),
            P("tower", "dev", None),
            P("tower", "dev"),
            P("tower", "dev", None),
            P("tower", "dev"),
            P(("tower", "dev"), None),
            P(("tower", "dev"), None),
            P(("tower", "dev")),
            P(("tower", "dev")),
        ),
        check_vma=False,
    )
```

```python
import functools

import jax
import jax.numpy as jnp
from jax import lax
from jax.experimental import pallas as pl
from jax.experimental.pallas import tpu as pltpu
from jax.sharding import PartitionSpec as P

LOSS_SCALE = 1024
NC = 4
F32 = jnp.float32
BF16 = jnp.bfloat16
MESH = pl.DeviceIdType.MESH


def dot(a, b):
    return jnp.dot(a, b, preferred_element_type=F32)


def dot_t(a, b):
    return lax.dot_general(a, b, (((1,), (1,)), ((), ())), preferred_element_type=F32)


def kernel(
    dims,
    emb, tv_h, tu_h, cb, pw_h, pb, av_h, au_h, ab, lw, labels,
    emb_land, vw_out, uw_out, cb_out, pw_out, pb_out, gav_out, gau_out, gab_out, glw_out,
    base, tv, tu, pw, av, au,
    low, scale, mixed, sgrad, gpre, gcb, glow,
    out, arch_in, back_s, back_r, ag, eg,
    cb_acc, pb_acc, vec_acc,
    w_s, w_r, w_xs, w_xr, u_s, u_t, u_r, u_xr, a1_s, a1_r, a2_f, a2_s, a2_r,
    local_sem, fwd_ss, fwd_rs, out_ss, out_rs, back_ss, back_rs,
    agx_ss, agx_rs, agz_ss, agz_rs, agc_ss, agc_rs,
    emb_ss, emb_rs, w_ss, w_rs, wx_ss, wx_rs, u_ss, u_rs, ux_ss, ux_rs, a1_ss, a1_rs, a2_ss, a2_rs,
):
    T, D, SB, OC = dims["T"], dims["D"], dims["SB"], dims["OC"]
    HI = 2
    DY = D // HI
    SC = SB // NC
    R = T * SC
    W = D * OC
    RANK, PROJ, AR = dims["RANK"], dims["PROJ"], dims["AR"]
    ARCH = T * PROJ
    RR = RANK // D
    AP = PROJ // D
    UR = AR // T
    UF = UR // D
    t = lax.axis_index("tower")
    d = lax.axis_index("dev")
    d_hi = lax.div(d, DY)
    d_y = lax.rem(d, DY)
    t_zx = lax.div(t, 2)
    t_core = lax.rem(t, 2)
    t_z = lax.div(t, 4)
    t_zx_beside = 2 * t_z + 1 - lax.rem(t_zx, 2)

    def dev(k):
        k = lax.rem(k, 2) * DY + lax.div(k, 2)
        hi = lax.rem(d_hi + lax.div(k, DY), HI)
        return hi * DY + lax.rem(d_y + lax.rem(k, DY), DY)

    def tow(k):
        return lax.rem(t + k, T)

    def cols(j, n):
        if isinstance(j, int):
            return slice(j * n, (j + 1) * n)
        return pl.ds(pl.multiple_of(j * n, n), n)

    def loop(lo, hi, f):
        lax.fori_loop(lo, hi, lambda i, x: (f(i), x)[1], 0)

    def unrolled(lo, hi, f):
        for i in range(lo, hi):
            f(i)

    def remote(src, dst, ss, rs, who):
        return pltpu.make_async_remote_copy(
            src_ref=src, dst_ref=dst, send_sem=ss, recv_sem=rs, device_id=who, device_id_type=MESH
        )

    barrier = pltpu.get_barrier_semaphore()
    loop(1, D, lambda k: pl.semaphore_signal(
        barrier, inc=1, device_id=(t, dev(jnp.int32(k))), device_id_type=MESH))
    loop(1, T, lambda k: pl.semaphore_signal(
        barrier, inc=1, device_id=(tow(k), d), device_id_type=MESH))
    pl.semaphore_wait(barrier, D + T - 2)

    def fwd(c, k):
        j = dev(k)
        return remote(
            emb.at[:, j, pl.ds(c * SC, SC), :], base.at[c, :, :, cols(d, OC)],
            fwd_ss.at[c, k], fwd_rs.at[c, d], (t, j))

    def fwd_arrival(c, k):
        j = dev(k)
        return remote(
            emb.at[:, j, pl.ds(c * SC, SC), :], base.at[c, :, :, cols(j, OC)],
            fwd_ss.at[c, k], fwd_rs.at[c, j], (t, j))

    def tower_out(c, k):
        j = tow(k)
        return remote(
            out.at[c, j], arch_in.at[c, :, cols(t, PROJ)],
            out_ss.at[c, k], out_rs.at[c, t], (j, d))

    def tower_out_arrival(c, k):
        j = tow(k)
        return remote(
            out.at[c, j], arch_in.at[c, :, cols(j, PROJ)],
            out_ss.at[c, k], out_rs.at[c, j], (j, d))

    def back(c, k, who):
        j = tow(k)
        return remote(
            back_s.at[c, j], back_r.at[c, who], back_ss.at[c, k], back_rs.at[c, who], (j, d))

    def pair(c, z, core):
        return ag.at[c, pl.ds(2 * z, 2), core]

    def gather_x(c, own):
        zx = t_zx if own else t_zx_beside
        src = ag.at[c, t_zx, t_core]
        return remote(
            src, ag.at[c, zx, t_core], agx_ss.at[c], agx_rs.at[c],
            (2 * t_zx_beside + t_core, d))

    def gather_z(c, k, own):
        z = lax.rem(t_z + k, T // 4)
        who = t_z if own else z
        return remote(
            pair(c, t_z, t_core), pair(c, who, t_core), agz_ss.at[c, k], agz_rs.at[c, who],
            (4 * z + lax.rem(t, 4), d))

    def gather_core(c, own):
        core = t_core if own else 1 - t_core
        return remote(
            ag.at[c, :, t_core], ag.at[c, :, core], agc_ss.at[c], agc_rs.at[c],
            (2 * t_zx + 1 - t_core, d))

    def emb_back(c, k, who):
        j = dev(k)
        return remote(
            eg.at[c, j], emb_land.at[:, who, pl.ds(c * SC, SC), :],
            emb_ss.at[c, k], emb_rs.at[c, who], (t, j))

    def over_dev(s, r, ss, rs):
        def make(k, who):
            j = dev(k)
            return remote(s.at[j], r.at[who], ss.at[k], rs.at[who], (t, j))
        return make

    def along_y(s, r, ss, rs):
        def make(k, own):
            y = lax.rem(d_y + k, DY)
            who = d_y if own else y
            return remote(
                s.at[:, y], r.at[who], ss.at[k], rs.at[who], (t, d_hi * DY + y))
        return make

    def across_x(s, r, ss, rs):
        return remote(s, r, ss.at[0], rs.at[0], (t, (1 - d_hi) * DY + d_y))

    w_copy = along_y(w_s, w_r, w_ss, w_rs)

    def u_copy(k, own):
        y = lax.rem(d_y + k, DY)
        who = d_y if own else y
        return remote(
            u_t.at[y], u_r.at[who], u_ss.at[k], u_rs.at[who], (t, d_hi * DY + y))

    def w_across():
        return across_x(w_xs, w_xr, wx_ss, wx_rs)

    def u_across():
        return across_x(u_s.at[1 - d_hi], u_xr, ux_ss, ux_rs)

    def partial(r, hi):
        total = r[0, hi].astype(F32)
        for y in range(1, DY):
            total += r[y, hi].astype(F32)
        return total

    a2_copy = over_dev(a2_s, a2_r, a2_ss, a2_rs)

    def a1_copy(k, who):
        j = tow(k)
        return remote(a1_s.at[j], a1_r.at[who], a1_ss.at[k], a1_rs.at[who], (j, d))

    def fwd_own(c):
        return pltpu.make_async_copy(
            emb.at[:, d, pl.ds(c * SC, SC), :], base.at[c, :, :, cols(d, OC)], local_sem.at[c])

    def emb_own(c):
        return pltpu.make_async_copy(
            eg.at[c, d], emb_land.at[:, d, pl.ds(c * SC, SC), :], local_sem.at[NC + c])

    weights = [
        pltpu.make_async_copy(src, dst, local_sem.at[2 * NC + i])
        for i, (src, dst) in enumerate(
            [(tv_h, tv), (tu_h, tu), (pw_h, pw), (av_h, av), (au_h, au)])
    ]

    def start_fwd(c):
        loop(1, D, lambda k: fwd(c, k).start())

    for c in range(2):
        start_fwd(c)
    for w in weights:
        w.start()
    for c in range(NC):
        fwd_own(c).start()

    cb_acc[...] = jnp.zeros_like(cb_acc)
    pb_acc[...] = jnp.zeros_like(pb_acc)
    vec_acc[...] = jnp.zeros_like(vec_acc)
    for w in weights:
        w.wait()

    def forward(c):
        slot = lax.rem(c, 3)
        fwd_own(c).wait()
        loop(1, D, lambda k: fwd_arrival(c, k).wait_recv())
        low[c] = dot(base[c].reshape(R, W), tv[...]).astype(BF16)

        def forward_cols(j):
            at = cols(j, OC)
            s = dot(low[c], tu[:, at]) + (cb[:, at] + 1.0)
            scale[slot, :, at] = s
            b = base[c, :, :, at].reshape(R, OC).astype(F32)
            mixed[c, :, at] = (b * s).astype(BF16)

        unrolled(0, D, forward_cols)
        pre = dot(mixed[c], pw[...]) + pb[...]
        sig = jax.nn.sigmoid(pre)
        sgrad[slot] = sig * (1.0 + pre * (1.0 - sig))
        out[c] = (pre * sig).astype(BF16).reshape(T, SC, PROJ)
        loop(1, T, lambda k: tower_out(c, k).start())
        arch_in[c, :, cols(t, PROJ)] = out[c, t]

        @pl.when(c + 2 < NC)
        def _():
            start_fwd(c + 2)

    def over_arch(c):
        loop(1, T, lambda k: tower_out_arrival(c, k).wait_recv())
        a_in = arch_in[c]
        a_low = dot(a_in, av[...]).astype(BF16)
        a_scale = dot(a_low, au[...]) + (ab[...] + 1.0)
        a_f = a_in.astype(F32)
        mix = (a_f * a_scale).astype(BF16).astype(F32)
        logits = jnp.sum(mix * lw[...], axis=1, keepdims=True)
        row = lax.broadcasted_iota(jnp.int32, (SC, SB), 0) + c * SC
        lane = lax.broadcasted_iota(jnp.int32, (SC, SB), 1)
        label = jnp.sum(
            jnp.where(row == lane, jnp.broadcast_to(labels[...], (SC, SB)), 0.0),
            axis=1, keepdims=True)
        g = (jax.nn.sigmoid(logits) - label) * (LOSS_SCALE / (T * D * SB))
        g_mix = g * lw[...]
        g_cross = g_mix * a_f
        g_low = dot_t(g_cross.astype(BF16), au[...]).astype(BF16)
        g_in = (g_mix * a_scale + dot_t(g_low, av[...])).astype(BF16)
        for j in range(T):
            back_s[c, j] = g_in[:, j * PROJ:(j + 1) * PROJ]
        loop(1, T, lambda k: back(c, k, t).start())
        back_r[c, t] = back_s[c, t]
        ag[c, t_zx, t_core, :, 0:AR] = a_low
        ag[c, t_zx, t_core, :, AR:2 * AR] = g_low
        g_wide = jnp.broadcast_to(g, (SC, PROJ))
        g_high = g_wide.astype(BF16)
        ag[c, t_zx, t_core, :, 2 * AR:2 * AR + PROJ] = g_high
        ag[c, t_zx, t_core, :, 2 * AR + PROJ:] = (g_wide - g_high.astype(F32)).astype(BF16)
        gather_x(c, True).start()
        vec_acc[0:1, :] += jnp.sum(g_cross, axis=0, keepdims=True)
        vec_acc[1:2, :] += jnp.sum(g * mix, axis=0, keepdims=True)

    def backward(c):
        slot = lax.rem(c, 3)
        loop(1, T, lambda k: back(c, k, tow(k)).wait_recv())
        gather_x(c, False).wait_recv()
        loop(1, T // 4, lambda k: gather_z(c, k, True).start())
        g_pre = back_r[c].reshape(R, PROJ).astype(F32) * sgrad[slot]
        pb_acc[...] += jnp.sum(g_pre, axis=0, keepdims=True)
        gpre[c] = g_pre.astype(BF16)

        def backward_cols(j):
            at = cols(j, OC)
            gm = dot_t(gpre[c], pw[at, :])
            gc = gm * base[c, :, :, at].reshape(R, OC).astype(F32)
            cb_acc[:, at] += jnp.sum(gc, axis=0, keepdims=True)
            gcb[c, :, at] = gc.astype(BF16)
            scale[slot, :, at] = gm * scale[slot, :, at]

        unrolled(0, D, backward_cols)
        glow[c] = dot_t(gcb[c], tu[...]).astype(BF16)

        def grad_cols(j):
            at = cols(j, OC)
            v = scale[slot, :, at] + dot_t(glow[c], tv[at, :])
            eg[c, j] = v.astype(BF16).reshape(T, SC, OC)

        def grad_send(k):
            grad_cols(dev(jnp.int32(k)))
            emb_back(c, jnp.int32(k), d).start()

        unrolled(1, D, grad_send)
        grad_cols(d)
        emb_own(c).start()

        @pl.when(c > 0)
        def _():
            gather_last(c - 1)

    def gather_last(c):
        loop(1, T // 4, lambda k: gather_z(c, k, False).wait_recv())
        gather_core(c, True).start()

    def step(i):
        @pl.when(i < NC)
        def _():
            forward(i)

        @pl.when(jnp.logical_and(i >= 1, i <= NC))
        def _():
            over_arch(i - 1)

        @pl.when(i >= 2)
        def _():
            backward(i - 2)

    loop(0, NC + 2, step)

    gather_last(NC - 1)
    N = NC * R
    low_t = low[...].reshape(N, RANK).T

    def u_cols(j):
        at = cols(j, OC)
        v = dot(low_t, gcb[:, :, at].reshape(N, OC))
        u_s[:, :, :, at] = v.astype(BF16).reshape(HI, DY, RR, OC)

    unrolled(0, D, u_cols)
    u_across().start()
    glow_t = glow[...].reshape(N, RANK).T
    gpre_t = gpre[...].reshape(N, PROJ).T
    first = lax.broadcasted_iota(jnp.int32, (16, OC), 0) == 0
    pb2 = jnp.broadcast_to(jnp.concatenate([pb_acc[...]] * (OC // PROJ), axis=1), (16, OC))

    def w_cols(j):
        at = cols(j, OC)
        hi, y = j // DY, j % DY
        w_s[hi, y, 0:RANK, :] = dot(glow_t, base[:, :, :, at].reshape(N, OC)).astype(BF16)
        w_s[hi, y, RANK:RANK + PROJ, :] = dot(gpre_t, mixed[:, :, at].reshape(N, OC)).astype(BF16)
        w_s[hi, y, RANK + PROJ:RANK + PROJ + 16, :] = jnp.where(
            first, jnp.broadcast_to(cb_acc[:, at], (16, OC)), pb2).astype(BF16)

    unrolled(0, D, w_cols)
    loop(1, DY, lambda k: w_copy(k, True).start())
    w_r[d_y] = w_s[:, d_y]

    loop(0, NC, lambda c: gather_core(c, False).wait_recv())
    outs = out[...].reshape(N, PROJ)
    factors = ag[...].reshape(N, 2 * AR + 2 * PROJ)
    g = factors[:, 2 * AR:2 * AR + PROJ].astype(F32) + factors[:, 2 * AR + PROJ:].astype(F32)
    g_cross_t = (g * lw[:, cols(t, PROJ)] * outs.astype(F32)).astype(BF16).T
    gau = dot(g_cross_t, factors[:, :AR]).T
    zeros = jnp.zeros((8, PROJ), F32)
    for j in range(T):
        a1_s[j, 0:UR, :] = gau[j * UR:(j + 1) * UR, :].astype(BF16)
        a1_s[j, UR:UR + 16, :] = jnp.concatenate(
            [vec_acc[:, j * PROJ:(j + 1) * PROJ], zeros], axis=0).astype(BF16)
    loop(1, T, lambda k: a1_copy(k, t).start())
    a1_r[t] = a1_s[t]


    u_across().wait_recv()
    u_t[...] = (u_s[d_hi].astype(F32) + u_xr[...].astype(F32)).astype(BF16)
    loop(1, DY, lambda k: u_copy(k, True).start())
    u_r[d_y] = u_t[d_y]

    gav = dot(outs.T, factors[:, AR:2 * AR])
    half = ARCH // 2
    for j in range(D):
        a2_f[j, 8:16, 0:AR] = gav[j * AP:j * AP + 8, :]
        a2_f[j, 8:16, AR:2 * AR] = gav[j * AP + 8:j * AP + 16, :]
    loop(1, T, lambda k: a1_copy(k, tow(k)).wait_recv())
    vec = jnp.sum(a1_r[:, UR:UR + 16, :].astype(F32), axis=0)
    per = half // PROJ
    for i in range(T):
        part = a1_r[i, 0:UR, :].astype(F32)
        r0 = UF * (i // per)
        c0 = (i % per) * PROJ
        for j in range(D):
            a2_f[j, r0:r0 + UF, c0:c0 + PROJ] = part[j * UF:(j + 1) * UF, :]
    for j in range(D):
        a2_f[j, :, half:half + PROJ] = vec
    a2_s[...] = a2_f[...].astype(BF16)
    loop(1, D, lambda k: a2_copy(k, d).start())
    a2_r[d] = a2_s[d]

    loop(1, DY, lambda k: w_copy(k, False).wait_recv())
    w_xs[...] = partial(w_r, 1 - d_hi).astype(BF16)
    w_across().start()
    loop(1, DY, lambda k: u_copy(k, False).wait_recv())
    uw_out[...] = jnp.sum(u_r[...].astype(F32), axis=0)
    w_own = partial(w_r, d_hi)
    w_across().wait_recv()
    ws = w_own + w_xr[...].astype(F32)
    vw_out[...] = ws[0:RANK].T
    pw_out[...] = ws[RANK:RANK + PROJ].T
    cb_out[...] = ws[RANK + PROJ:RANK + PROJ + 1]
    shift = lax.rem(PROJ - d * AP, PROJ)
    vec = pltpu.roll(ws[RANK + PROJ + 8:RANK + PROJ + 16, 0:PROJ], shift, 1)
    pb_out[...] = vec[0:1, 0:AP]

    loop(1, D, lambda k: a2_copy(k, dev(k)).wait_recv())
    a2 = jnp.sum(a2_r[...].astype(F32), axis=0)
    gau_out[:, 0:half] = a2[0:UF, 0:half]
    gau_out[:, half:] = a2[UF:2 * UF, 0:half]
    gav_out[0:8, :] = a2[8:16, 0:AR]
    gav_out[8:16, :] = a2[8:16, AR:2 * AR]
    vec = pltpu.roll(a2[0:8, half:half + PROJ], shift, 1)
    gab_out[...] = vec[0:1, 0:AP]
    glw_out[...] = vec[1:2, 0:AP]

    for c in range(NC):
        emb_own(c).wait()

        def drain_dev(k):
            fwd(c, k).wait_send()
            emb_back(c, k, d).wait_send()
            emb_back(c, k, dev(k)).wait_recv()

        def drain_tower(k):
            tower_out(c, k).wait_send()
            back(c, k, t).wait_send()

        gather_x(c, True).wait_send()
        gather_core(c, True).wait_send()
        loop(1, T // 4, lambda k: gather_z(c, k, True).wait_send())
        loop(1, D, drain_dev)
        loop(1, T, drain_tower)

    def drain_last(k):
        a2_copy(k, d).wait_send()

    loop(1, D, drain_last)

    def drain_weights(k):
        u_copy(k, True).wait_send()
        w_copy(k, True).wait_send()

    loop(1, DY, drain_weights)
    u_across().wait_send()
    w_across().wait_send()
    loop(1, T, lambda k: a1_copy(k, t).wait_send())


def deliver(n, *refs):
    src, dst, held, sem_in, sem_out = refs[:n], refs[n:2 * n], refs[2 * n:3 * n], refs[-2], refs[-1]
    parts = [(0, i) for i in range(src[0].shape[0])] + [(a, None) for a in range(1, n)]

    def at(ref, i):
        return ref if i is None else ref.at[i]

    into = [
        pltpu.make_async_copy(at(src[a], i), at(held[a], i), sem_in.at[k])
        for k, (a, i) in enumerate(parts)
    ]
    away = [
        pltpu.make_async_copy(at(held[a], i), at(dst[a], i), sem_out.at[k])
        for k, (a, i) in enumerate(parts)
    ]
    for copy in into:
        copy.start()
    for copy, onward in zip(into, away):
        copy.wait()
        onward.start()
    for copy in away:
        copy.wait()


def local(
    embeddings, tower_v, tower_u, cross_bias, proj_w, proj_bias,
    arch_v, arch_u, arch_bias, logit_w, labels,
):
    T = lax.axis_size("tower")
    D = lax.axis_size("dev")
    rows, OC = embeddings.shape
    SB = rows // (T * D)
    SC = SB // NC
    R = T * SC
    W = D * OC
    RANK = tower_v.shape[2]
    PROJ = proj_w.shape[2]
    ARCH, AR = arch_v.shape
    UR = AR // T
    AP = PROJ // D
    WR = RANK + PROJ + 16
    AGW = 2 * AR + 2 * PROJ
    A2 = ARCH // 2 + PROJ
    dims = dict(T=T, D=D, SB=SB, OC=OC, RANK=RANK, PROJ=PROJ, AR=AR)
    vmem = pl.BlockSpec(memory_space=pltpu.VMEM)
    hbm = pl.BlockSpec(memory_space=pl.ANY)
    dma = pltpu.SemaphoreType.DMA
    outs = pl.pallas_call(
        functools.partial(kernel, dims),
        out_shape=(
            jax.ShapeDtypeStruct((T, D, SB, OC), BF16),
            jax.ShapeDtypeStruct((W // D, RANK), F32),
            jax.ShapeDtypeStruct((RANK // D, W), F32),
            jax.ShapeDtypeStruct((1, OC), F32),
            jax.ShapeDtypeStruct((W // D, PROJ), F32),
            jax.ShapeDtypeStruct((1, AP), F32),
            jax.ShapeDtypeStruct((AP, AR), F32),
            jax.ShapeDtypeStruct((UR // D, ARCH), F32),
            jax.ShapeDtypeStruct((1, AP), F32),
            jax.ShapeDtypeStruct((1, AP), F32),
        ),
        in_specs=[hbm, hbm, hbm, vmem, hbm, vmem, hbm, hbm, vmem, vmem, vmem],
        out_specs=(hbm,) + (vmem,) * 9,
        scratch_shapes=[
            pltpu.VMEM((NC, T, SC, W), BF16),
            pltpu.VMEM((W, RANK), BF16),
            pltpu.VMEM((RANK, W), BF16),
            pltpu.VMEM((W, PROJ), BF16),
            pltpu.VMEM((ARCH, AR), BF16),
            pltpu.VMEM((AR, ARCH), BF16),
            pltpu.VMEM((NC, R, RANK), BF16),
            pltpu.VMEM((3, R, W), F32),
            pltpu.VMEM((NC, R, W), BF16),
            pltpu.VMEM((3, R, PROJ), F32),
            pltpu.VMEM((NC, R, PROJ), BF16),
            pltpu.VMEM((NC, R, W), BF16),
            pltpu.VMEM((NC, R, RANK), BF16),
            pltpu.VMEM((NC, T, SC, PROJ), BF16),
            pltpu.VMEM((NC, SC, ARCH), BF16),
            pltpu.VMEM((NC, T, SC, PROJ), BF16),
            pltpu.VMEM((NC, T, SC, PROJ), BF16),
            pltpu.VMEM((NC, T // 2, 2, SC, AGW), BF16),
            pltpu.VMEM((NC, D, T, SC, OC), BF16),
            pltpu.VMEM((1, W), F32),
            pltpu.VMEM((1, PROJ), F32),
            pltpu.VMEM((8, ARCH), F32),
            pltpu.VMEM((2, D // 2, WR, OC), BF16),
            pltpu.VMEM((D // 2, 2, WR, OC), BF16),
            pltpu.VMEM((WR, OC), BF16),
            pltpu.VMEM((WR, OC), BF16),
            pltpu.VMEM((2, D // 2, RANK // D, W), BF16),
            pltpu.VMEM((D // 2, RANK // D, W), BF16),
            pltpu.VMEM((D // 2, RANK // D, W), BF16),
            pltpu.VMEM((D // 2, RANK // D, W), BF16),
            pltpu.VMEM((T, UR + 16, PROJ), BF16),
            pltpu.VMEM((T, UR + 16, PROJ), BF16),
            pltpu.VMEM((D, 16, A2), F32),
            pltpu.VMEM((D, 16, A2), BF16),
            pltpu.VMEM((D, 16, A2), BF16),
            dma((2 * NC + 5,)),
            dma((NC, D)), dma((NC, D)),
            dma((NC, T)), dma((NC, T)),
            dma((NC, T)), dma((NC, T)),
            dma((NC,)), dma((NC,)),
            dma((NC, T // 4)), dma((NC, T // 4)),
            dma((NC,)), dma((NC,)),
            dma((NC, D)), dma((NC, D)),
            dma((D // 2,)), dma((D // 2,)), dma((1,)), dma((1,)),
            dma((D // 2,)), dma((D // 2,)), dma((1,)), dma((1,)),
            dma((T,)), dma((T,)),
            dma((D,)), dma((D,)),
        ],
        compiler_params=pltpu.CompilerParams(
            collective_id=0, has_side_effects=True, vmem_limit_bytes=60 << 20
        ),
    )(
        embeddings.reshape(T, D, SB, OC), tower_v[0], tower_u[0], cross_bias, proj_w[0], proj_bias,
        arch_v, arch_u, arch_bias[None], logit_w[None], labels[None],
    )
    n = len(outs)
    eg, vw, uw, cb, pw, pb, gav, gau, gab, glw = pl.pallas_call(
        functools.partial(deliver, n),
        out_shape=tuple(jax.ShapeDtypeStruct(x.shape, x.dtype) for x in outs),
        in_specs=[hbm] * n,
        out_specs=(hbm,) * n,
        scratch_shapes=[pltpu.VMEM(x.shape, x.dtype) for x in outs]
        + [dma((T + n - 1,)), dma((T + n - 1,))],
        compiler_params=pltpu.CompilerParams(vmem_limit_bytes=60 << 20),
    )(*outs)
    return (
        eg.reshape(rows, OC), vw[None], uw[None], cb, pw[None], pb,
        gav, gau, gab[0], glw[0],
    )


def solution(mesh):
    return jax.shard_map(
        local,
        mesh=mesh,
        in_specs=(
            P(None, ("tower", "dev")),
            P("tower", None, None),
            P("tower", None, None),
            P("tower", None),
            P("tower", None, None),
            P("tower", None),
            P(),
            P(),
            P(),
            P(),
            P(("tower", "dev")),
        ),
        out_specs=(
            P(None, ("tower", "dev")),
            P("tower", "dev", None),
            P("tower", "dev", None),
            P("tower", "dev"),
            P("tower", "dev", None),
            P("tower", "dev"),
            P(("tower", "dev"), None),
            P(("tower", "dev"), None),
            P(("tower", "dev")),
            P(("tower", "dev")),
        ),
        check_vma=False,
    )
```

```python
import functools

import jax
import jax.numpy as jnp
from jax import lax
from jax.experimental import pallas as pl
from jax.experimental.pallas import tpu as pltpu
from jax.sharding import PartitionSpec as P

LOSS_SCALE = 1024
NC = 4
F32 = jnp.float32
BF16 = jnp.bfloat16
MESH = pl.DeviceIdType.MESH


def dot(a, b):
    return jnp.dot(a, b, preferred_element_type=F32)


def dot_t(a, b):
    return lax.dot_general(a, b, (((1,), (1,)), ((), ())), preferred_element_type=F32)


def kernel(
    dims,
    emb, tv_h, tu_h, cb, pw_h, pb, av_h, au_h, ab, lw, labels,
    emb_land, vw_out, uw_out, cb_out, pw_out, pb_out, gav_out, gau_out, gab_out, glw_out,
    base, tv, tu, pw, av, au,
    low, scale, mixed, sgrad, gpre, gcb, glow,
    out, arch_in, back_s, back_r, ag, eg,
    cb_acc, pb_acc, vec_acc,
    w_s, w_r, w_xs, w_xr, p_s, p_r, p_xs, p_xr, u_s, u_t, u_r, u_xr, a1_s, a1_r, a2_f, a2_s, a2_r,
    local_sem, fwd_ss, fwd_rs, out_ss, out_rs, back_ss, back_rs,
    agx_ss, agx_rs, agz_ss, agz_rs, agc_ss, agc_rs,
    emb_ss, emb_rs, w_ss, w_rs, wx_ss, wx_rs, p_ss, p_rs, px_ss, px_rs, u_ss, u_rs, ux_ss, ux_rs, a1_ss, a1_rs, a2_ss, a2_rs,
):
    T, D, SB, OC = dims["T"], dims["D"], dims["SB"], dims["OC"]
    HI = 2
    DY = D // HI
    SC = SB // NC
    R = T * SC
    W = D * OC
    RANK, PROJ, AR = dims["RANK"], dims["PROJ"], dims["AR"]
    ARCH = T * PROJ
    RR = RANK // D
    AP = PROJ // D
    UR = AR // T
    UF = UR // D
    t = lax.axis_index("tower")
    d = lax.axis_index("dev")
    d_hi = lax.div(d, DY)
    d_y = lax.rem(d, DY)
    t_zx = lax.div(t, 2)
    t_core = lax.rem(t, 2)
    t_z = lax.div(t, 4)
    t_zx_beside = 2 * t_z + 1 - lax.rem(t_zx, 2)

    def dev(k):
        k = lax.rem(k, 2) * DY + lax.div(k, 2)
        hi = lax.rem(d_hi + lax.div(k, DY), HI)
        return hi * DY + lax.rem(d_y + lax.rem(k, DY), DY)

    def tow(k):
        return lax.rem(t + k, T)

    def cols(j, n):
        if isinstance(j, int):
            return slice(j * n, (j + 1) * n)
        return pl.ds(pl.multiple_of(j * n, n), n)

    def loop(lo, hi, f):
        lax.fori_loop(lo, hi, lambda i, x: (f(i), x)[1], 0)

    def unrolled(lo, hi, f):
        for i in range(lo, hi):
            f(i)

    def remote(src, dst, ss, rs, who):
        return pltpu.make_async_remote_copy(
            src_ref=src, dst_ref=dst, send_sem=ss, recv_sem=rs, device_id=who, device_id_type=MESH
        )

    barrier = pltpu.get_barrier_semaphore()
    loop(1, D, lambda k: pl.semaphore_signal(
        barrier, inc=1, device_id=(t, dev(jnp.int32(k))), device_id_type=MESH))
    loop(1, T, lambda k: pl.semaphore_signal(
        barrier, inc=1, device_id=(tow(k), d), device_id_type=MESH))
    pl.semaphore_wait(barrier, D + T - 2)

    def fwd(c, k):
        j = dev(k)
        return remote(
            emb.at[:, j, pl.ds(c * SC, SC), :], base.at[c, :, :, cols(d, OC)],
            fwd_ss.at[c, k], fwd_rs.at[c, d], (t, j))

    def fwd_arrival(c, k):
        j = dev(k)
        return remote(
            emb.at[:, j, pl.ds(c * SC, SC), :], base.at[c, :, :, cols(j, OC)],
            fwd_ss.at[c, k], fwd_rs.at[c, j], (t, j))

    def tower_out(c, k):
        j = tow(k)
        return remote(
            out.at[c, j], arch_in.at[c, :, cols(t, PROJ)],
            out_ss.at[c, k], out_rs.at[c, t], (j, d))

    def tower_out_arrival(c, k):
        j = tow(k)
        return remote(
            out.at[c, j], arch_in.at[c, :, cols(j, PROJ)],
            out_ss.at[c, k], out_rs.at[c, j], (j, d))

    def back(c, k, who):
        j = tow(k)
        return remote(
            back_s.at[c, j], back_r.at[c, who], back_ss.at[c, k], back_rs.at[c, who], (j, d))

    def pair(c, z, core):
        return ag.at[c, pl.ds(2 * z, 2), core]

    def gather_x(c, own):
        zx = t_zx if own else t_zx_beside
        src = ag.at[c, t_zx, t_core]
        return remote(
            src, ag.at[c, zx, t_core], agx_ss.at[c], agx_rs.at[c],
            (2 * t_zx_beside + t_core, d))

    def gather_z(c, k, own):
        z = lax.rem(t_z + k, T // 4)
        who = t_z if own else z
        return remote(
            pair(c, t_z, t_core), pair(c, who, t_core), agz_ss.at[c, k], agz_rs.at[c, who],
            (4 * z + lax.rem(t, 4), d))

    def gather_core(c, own):
        core = t_core if own else 1 - t_core
        return remote(
            ag.at[c, :, t_core], ag.at[c, :, core], agc_ss.at[c], agc_rs.at[c],
            (2 * t_zx + 1 - t_core, d))

    def emb_back(c, k, who):
        j = dev(k)
        return remote(
            eg.at[c, j], emb_land.at[:, who, pl.ds(c * SC, SC), :],
            emb_ss.at[c, k], emb_rs.at[c, who], (t, j))

    def over_dev(s, r, ss, rs):
        def make(k, who):
            j = dev(k)
            return remote(s.at[j], r.at[who], ss.at[k], rs.at[who], (t, j))
        return make

    def along_y(s, r, ss, rs):
        def make(k, own):
            y = lax.rem(d_y + k, DY)
            who = d_y if own else y
            return remote(
                s.at[:, y], r.at[who], ss.at[k], rs.at[who], (t, d_hi * DY + y))
        return make

    def across_x(s, r, ss, rs):
        return remote(s, r, ss.at[0], rs.at[0], (t, (1 - d_hi) * DY + d_y))

    w_copy = along_y(w_s, w_r, w_ss, w_rs)
    p_copy = along_y(p_s, p_r, p_ss, p_rs)

    def u_copy(k, own):
        y = lax.rem(d_y + k, DY)
        who = d_y if own else y
        return remote(
            u_t.at[y], u_r.at[who], u_ss.at[k], u_rs.at[who], (t, d_hi * DY + y))

    def p_across():
        return across_x(p_xs, p_xr, px_ss, px_rs)

    def w_across():
        return across_x(w_xs, w_xr, wx_ss, wx_rs)

    def u_across():
        return across_x(u_s.at[1 - d_hi], u_xr, ux_ss, ux_rs)

    def partial(r, hi):
        total = r[0, hi].astype(F32)
        for y in range(1, DY):
            total += r[y, hi].astype(F32)
        return total

    a2_copy = over_dev(a2_s, a2_r, a2_ss, a2_rs)

    def a1_copy(k, who):
        j = tow(k)
        return remote(a1_s.at[j], a1_r.at[who], a1_ss.at[k], a1_rs.at[who], (j, d))

    def fwd_own(c):
        return pltpu.make_async_copy(
            emb.at[:, d, pl.ds(c * SC, SC), :], base.at[c, :, :, cols(d, OC)], local_sem.at[c])

    def emb_own(c):
        return pltpu.make_async_copy(
            eg.at[c, d], emb_land.at[:, d, pl.ds(c * SC, SC), :], local_sem.at[NC + c])

    weights = [
        pltpu.make_async_copy(src, dst, local_sem.at[2 * NC + i])
        for i, (src, dst) in enumerate(
            [(tv_h, tv), (tu_h, tu), (pw_h, pw), (av_h, av), (au_h, au)])
    ]

    def start_fwd(c):
        loop(1, D, lambda k: fwd(c, k).start())

    for c in range(2):
        start_fwd(c)
    for w in weights:
        w.start()
    for c in range(NC):
        fwd_own(c).start()

    cb_acc[...] = jnp.zeros_like(cb_acc)
    pb_acc[...] = jnp.zeros_like(pb_acc)
    vec_acc[...] = jnp.zeros_like(vec_acc)
    for w in weights:
        w.wait()

    def forward(c):
        slot = lax.rem(c, 4)
        fwd_own(c).wait()
        loop(1, D, lambda k: fwd_arrival(c, k).wait_recv())
        low[c] = dot(base[c].reshape(R, W), tv[...]).astype(BF16)

        def forward_cols(j):
            at = cols(j, OC)
            s = dot(low[c], tu[:, at]) + (cb[:, at] + 1.0)
            scale[slot, :, at] = s
            b = base[c, :, :, at].reshape(R, OC).astype(F32)
            mixed[c, :, at] = (b * s).astype(BF16)

        unrolled(0, D, forward_cols)
        pre = dot(mixed[c], pw[...]) + pb[...]
        sig = jax.nn.sigmoid(pre)
        sgrad[slot] = sig * (1.0 + pre * (1.0 - sig))
        out[c] = (pre * sig).astype(BF16).reshape(T, SC, PROJ)
        loop(1, T, lambda k: tower_out(c, k).start())
        arch_in[c, :, cols(t, PROJ)] = out[c, t]

        @pl.when(c + 2 < NC)
        def _():
            start_fwd(c + 2)

    def over_arch(c):
        loop(1, T, lambda k: tower_out_arrival(c, k).wait_recv())
        a_in = arch_in[c]
        a_low = dot(a_in, av[...]).astype(BF16)
        a_scale = dot(a_low, au[...]) + (ab[...] + 1.0)
        a_f = a_in.astype(F32)
        mix = (a_f * a_scale).astype(BF16).astype(F32)
        logits = jnp.sum(mix * lw[...], axis=1, keepdims=True)
        row = lax.broadcasted_iota(jnp.int32, (SC, SB), 0) + c * SC
        lane = lax.broadcasted_iota(jnp.int32, (SC, SB), 1)
        label = jnp.sum(
            jnp.where(row == lane, jnp.broadcast_to(labels[...], (SC, SB)), 0.0),
            axis=1, keepdims=True)
        g = (jax.nn.sigmoid(logits) - label) * (LOSS_SCALE / (T * D * SB))
        g_mix = g * lw[...]
        g_cross = g_mix * a_f
        g_low = dot_t(g_cross.astype(BF16), au[...]).astype(BF16)
        g_in = (g_mix * a_scale + dot_t(g_low, av[...])).astype(BF16)
        for j in range(T):
            back_s[c, j] = g_in[:, j * PROJ:(j + 1) * PROJ]
        loop(1, T, lambda k: back(c, k, t).start())
        back_r[c, t] = back_s[c, t]
        ag[c, t_zx, t_core, :, 0:AR] = a_low
        ag[c, t_zx, t_core, :, AR:2 * AR] = g_low
        g_wide = jnp.broadcast_to(g, (SC, PROJ))
        g_high = g_wide.astype(BF16)
        ag[c, t_zx, t_core, :, 2 * AR:2 * AR + PROJ] = g_high
        ag[c, t_zx, t_core, :, 2 * AR + PROJ:] = (g_wide - g_high.astype(F32)).astype(BF16)
        gather_x(c, True).start()
        vec_acc[0:1, :] += jnp.sum(g_cross, axis=0, keepdims=True)
        vec_acc[1:2, :] += jnp.sum(g * mix, axis=0, keepdims=True)

    def backward(c):
        slot = lax.rem(c, 4)
        loop(1, T, lambda k: back(c, k, tow(k)).wait_recv())
        gather_x(c, False).wait_recv()
        loop(1, T // 4, lambda k: gather_z(c, k, True).start())
        g_pre = back_r[c].reshape(R, PROJ).astype(F32) * sgrad[slot]
        pb_acc[...] += jnp.sum(g_pre, axis=0, keepdims=True)
        gpre[c] = g_pre.astype(BF16)

        def backward_cols(j):
            at = cols(j, OC)
            gm = dot_t(gpre[c], pw[at, :])
            gc = gm * base[c, :, :, at].reshape(R, OC).astype(F32)
            cb_acc[:, at] += jnp.sum(gc, axis=0, keepdims=True)
            gcb[c, :, at] = gc.astype(BF16)
            scale[slot, :, at] = gm * scale[slot, :, at]

        unrolled(0, D, backward_cols)
        glow[c] = dot_t(gcb[c], tu[...]).astype(BF16)

        def grad_cols(j):
            at = cols(j, OC)
            v = scale[slot, :, at] + dot_t(glow[c], tv[at, :])
            eg[c, j] = v.astype(BF16).reshape(T, SC, OC)

        def grad_send(k):
            grad_cols(dev(jnp.int32(k)))
            emb_back(c, jnp.int32(k), d).start()

        unrolled(1, D, grad_send)
        grad_cols(d)
        emb_own(c).start()

        @pl.when(c > 0)
        def _():
            gather_last(c - 1)

    def gather_last(c):
        loop(1, T // 4, lambda k: gather_z(c, k, False).wait_recv())
        gather_core(c, True).start()

    def step(i):
        @pl.when(i < NC)
        def _():
            forward(i)

        @pl.when(jnp.logical_and(i >= 1, i <= NC))
        def _():
            over_arch(i - 1)

        @pl.when(i >= 3)
        def _():
            backward(i - 3)

    loop(0, NC + 3, step)

    gather_last(NC - 1)
    N = NC * R
    glow_t = glow[...].reshape(N, RANK).T
    gpre_t = gpre[...].reshape(N, PROJ).T
    first = lax.broadcasted_iota(jnp.int32, (16, OC), 0) == 0
    pb2 = jnp.broadcast_to(jnp.concatenate([pb_acc[...]] * (OC // PROJ), axis=1), (16, OC))

    def w_cols(j):
        at = cols(j, OC)
        hi, y = j // DY, j % DY
        w_s[hi, y] = dot(glow_t, base[:, :, :, at].reshape(N, OC)).astype(BF16)

    def p_cols(j):
        at = cols(j, OC)
        hi, y = j // DY, j % DY
        p_s[hi, y, 0:PROJ, :] = dot(gpre_t, mixed[:, :, at].reshape(N, OC)).astype(BF16)
        p_s[hi, y, PROJ:PROJ + 16, :] = jnp.where(
            first, jnp.broadcast_to(cb_acc[:, at], (16, OC)), pb2).astype(BF16)

    unrolled(0, D, w_cols)
    loop(1, DY, lambda k: w_copy(k, True).start())
    w_r[d_y] = w_s[:, d_y]
    unrolled(0, D, p_cols)
    loop(1, DY, lambda k: p_copy(k, True).start())
    p_r[d_y] = p_s[:, d_y]

    loop(0, NC, lambda c: gather_core(c, False).wait_recv())
    outs = out[...].reshape(N, PROJ)
    factors = ag[...].reshape(N, 2 * AR + 2 * PROJ)
    g = factors[:, 2 * AR:2 * AR + PROJ].astype(F32) + factors[:, 2 * AR + PROJ:].astype(F32)
    g_cross_t = (g * lw[:, cols(t, PROJ)] * outs.astype(F32)).astype(BF16).T
    gau = dot(g_cross_t, factors[:, :AR]).T
    zeros = jnp.zeros((8, PROJ), F32)
    for j in range(T):
        a1_s[j, 0:UR, :] = gau[j * UR:(j + 1) * UR, :].astype(BF16)
        a1_s[j, UR:UR + 16, :] = jnp.concatenate(
            [vec_acc[:, j * PROJ:(j + 1) * PROJ], zeros], axis=0).astype(BF16)
    loop(1, T, lambda k: a1_copy(k, t).start())
    a1_r[t] = a1_s[t]
    low_t = low[...].reshape(N, RANK).T

    def u_cols(j):
        at = cols(j, OC)
        v = dot(low_t, gcb[:, :, at].reshape(N, OC))
        u_s[:, :, :, at] = v.astype(BF16).reshape(HI, DY, RR, OC)

    unrolled(0, D, u_cols)
    u_across().start()


    half = ARCH // 2
    gav = dot(outs.T, factors[:, AR:2 * AR])
    for j in range(D):
        a2_f[j, 8:16, 0:AR] = gav[j * AP:j * AP + 8, :]
        a2_f[j, 8:16, AR:2 * AR] = gav[j * AP + 8:j * AP + 16, :]
    loop(1, T, lambda k: a1_copy(k, tow(k)).wait_recv())
    vec = jnp.sum(a1_r[:, UR:UR + 16, :].astype(F32), axis=0)
    per = half // PROJ
    for i in range(T):
        part = a1_r[i, 0:UR, :].astype(F32)
        r0 = UF * (i // per)
        c0 = (i % per) * PROJ
        for j in range(D):
            a2_f[j, r0:r0 + UF, c0:c0 + PROJ] = part[j * UF:(j + 1) * UF, :]
    for j in range(D):
        a2_f[j, :, half:half + PROJ] = vec
    a2_s[...] = a2_f[...].astype(BF16)
    loop(1, D, lambda k: a2_copy(k, d).start())
    a2_r[d] = a2_s[d]
    u_across().wait_recv()
    u_t[...] = (u_s[d_hi].astype(F32) + u_xr[...].astype(F32)).astype(BF16)
    loop(1, DY, lambda k: u_copy(k, True).start())
    u_r[d_y] = u_t[d_y]


    loop(1, DY, lambda k: w_copy(k, False).wait_recv())
    w_xs[...] = partial(w_r, 1 - d_hi).astype(BF16)
    w_across().start()
    loop(1, DY, lambda k: p_copy(k, False).wait_recv())
    p_xs[...] = partial(p_r, 1 - d_hi).astype(BF16)
    p_across().start()
    loop(1, DY, lambda k: u_copy(k, False).wait_recv())
    uw_out[...] = jnp.sum(u_r[...].astype(F32), axis=0)
    w_own = partial(w_r, d_hi)
    w_across().wait_recv()
    vw_out[...] = (w_own + w_xr[...].astype(F32)).T
    p_own = partial(p_r, d_hi)
    p_across().wait_recv()
    ps = p_own + p_xr[...].astype(F32)
    pw_out[...] = ps[0:PROJ].T
    cb_out[...] = ps[PROJ:PROJ + 1]
    shift = lax.rem(PROJ - d * AP, PROJ)
    vec = pltpu.roll(ps[PROJ + 8:PROJ + 16, 0:PROJ], shift, 1)
    pb_out[...] = vec[0:1, 0:AP]

    loop(1, D, lambda k: a2_copy(k, dev(k)).wait_recv())
    a2 = jnp.sum(a2_r[...].astype(F32), axis=0)
    gau_out[:, 0:half] = a2[0:UF, 0:half]
    gau_out[:, half:] = a2[UF:2 * UF, 0:half]
    gav_out[0:8, :] = a2[8:16, 0:AR]
    gav_out[8:16, :] = a2[8:16, AR:2 * AR]
    vec = pltpu.roll(a2[0:8, half:half + PROJ], shift, 1)
    gab_out[...] = vec[0:1, 0:AP]
    glw_out[...] = vec[1:2, 0:AP]

    for c in range(NC):
        emb_own(c).wait()

        def drain_dev(k):
            fwd(c, k).wait_send()
            emb_back(c, k, d).wait_send()
            emb_back(c, k, dev(k)).wait_recv()

        def drain_tower(k):
            tower_out(c, k).wait_send()
            back(c, k, t).wait_send()

        gather_x(c, True).wait_send()
        gather_core(c, True).wait_send()
        loop(1, T // 4, lambda k: gather_z(c, k, True).wait_send())
        loop(1, D, drain_dev)
        loop(1, T, drain_tower)

    def drain_last(k):
        a2_copy(k, d).wait_send()

    loop(1, D, drain_last)

    def drain_weights(k):
        u_copy(k, True).wait_send()
        w_copy(k, True).wait_send()
        p_copy(k, True).wait_send()

    loop(1, DY, drain_weights)
    u_across().wait_send()
    w_across().wait_send()
    p_across().wait_send()
    loop(1, T, lambda k: a1_copy(k, t).wait_send())


def deliver(n, *refs):
    src, dst, held, sem_in, sem_out = refs[:n], refs[n:2 * n], refs[2 * n:3 * n], refs[-2], refs[-1]
    parts = [(0, i) for i in range(src[0].shape[0])] + [(a, None) for a in range(1, n)]

    def at(ref, i):
        return ref if i is None else ref.at[i]

    into = [
        pltpu.make_async_copy(at(src[a], i), at(held[a], i), sem_in.at[k])
        for k, (a, i) in enumerate(parts)
    ]
    away = [
        pltpu.make_async_copy(at(held[a], i), at(dst[a], i), sem_out.at[k])
        for k, (a, i) in enumerate(parts)
    ]
    for copy in into:
        copy.start()
    for copy, onward in zip(into, away):
        copy.wait()
        onward.start()
    for copy in away:
        copy.wait()


def local(
    embeddings, tower_v, tower_u, cross_bias, proj_w, proj_bias,
    arch_v, arch_u, arch_bias, logit_w, labels,
):
    T = lax.axis_size("tower")
    D = lax.axis_size("dev")
    rows, OC = embeddings.shape
    SB = rows // (T * D)
    SC = SB // NC
    R = T * SC
    W = D * OC
    RANK = tower_v.shape[2]
    PROJ = proj_w.shape[2]
    ARCH, AR = arch_v.shape
    UR = AR // T
    AP = PROJ // D
    PR = PROJ + 16
    AGW = 2 * AR + 2 * PROJ
    A2 = ARCH // 2 + PROJ
    dims = dict(T=T, D=D, SB=SB, OC=OC, RANK=RANK, PROJ=PROJ, AR=AR)
    vmem = pl.BlockSpec(memory_space=pltpu.VMEM)
    hbm = pl.BlockSpec(memory_space=pl.ANY)
    dma = pltpu.SemaphoreType.DMA
    outs = pl.pallas_call(
        functools.partial(kernel, dims),
        out_shape=(
            jax.ShapeDtypeStruct((T, D, SB, OC), BF16),
            jax.ShapeDtypeStruct((W // D, RANK), F32),
            jax.ShapeDtypeStruct((RANK // D, W), F32),
            jax.ShapeDtypeStruct((1, OC), F32),
            jax.ShapeDtypeStruct((W // D, PROJ), F32),
            jax.ShapeDtypeStruct((1, AP), F32),
            jax.ShapeDtypeStruct((AP, AR), F32),
            jax.ShapeDtypeStruct((UR // D, ARCH), F32),
            jax.ShapeDtypeStruct((1, AP), F32),
            jax.ShapeDtypeStruct((1, AP), F32),
        ),
        in_specs=[hbm, hbm, hbm, vmem, hbm, vmem, hbm, hbm, vmem, vmem, vmem],
        out_specs=(hbm,) + (vmem,) * 9,
        scratch_shapes=[
            pltpu.VMEM((NC, T, SC, W), BF16),
            pltpu.VMEM((W, RANK), BF16),
            pltpu.VMEM((RANK, W), BF16),
            pltpu.VMEM((W, PROJ), BF16),
            pltpu.VMEM((ARCH, AR), BF16),
            pltpu.VMEM((AR, ARCH), BF16),
            pltpu.VMEM((NC, R, RANK), BF16),
            pltpu.VMEM((4, R, W), F32),
            pltpu.VMEM((NC, R, W), BF16),
            pltpu.VMEM((4, R, PROJ), F32),
            pltpu.VMEM((NC, R, PROJ), BF16),
            pltpu.VMEM((NC, R, W), BF16),
            pltpu.VMEM((NC, R, RANK), BF16),
            pltpu.VMEM((NC, T, SC, PROJ), BF16),
            pltpu.VMEM((NC, SC, ARCH), BF16),
            pltpu.VMEM((NC, T, SC, PROJ), BF16),
            pltpu.VMEM((NC, T, SC, PROJ), BF16),
            pltpu.VMEM((NC, T // 2, 2, SC, AGW), BF16),
            pltpu.VMEM((NC, D, T, SC, OC), BF16),
            pltpu.VMEM((1, W), F32),
            pltpu.VMEM((1, PROJ), F32),
            pltpu.VMEM((8, ARCH), F32),
            pltpu.VMEM((2, D // 2, RANK, OC), BF16),
            pltpu.VMEM((D // 2, 2, RANK, OC), BF16),
            pltpu.VMEM((RANK, OC), BF16),
            pltpu.VMEM((RANK, OC), BF16),
            pltpu.VMEM((2, D // 2, PR, OC), BF16),
            pltpu.VMEM((D // 2, 2, PR, OC), BF16),
            pltpu.VMEM((PR, OC), BF16),
            pltpu.VMEM((PR, OC), BF16),
            pltpu.VMEM((2, D // 2, RANK // D, W), BF16),
            pltpu.VMEM((D // 2, RANK // D, W), BF16),
            pltpu.VMEM((D // 2, RANK // D, W), BF16),
            pltpu.VMEM((D // 2, RANK // D, W), BF16),
            pltpu.VMEM((T, UR + 16, PROJ), BF16),
            pltpu.VMEM((T, UR + 16, PROJ), BF16),
            pltpu.VMEM((D, 16, A2), F32),
            pltpu.VMEM((D, 16, A2), BF16),
            pltpu.VMEM((D, 16, A2), BF16),
            dma((2 * NC + 5,)),
            dma((NC, D)), dma((NC, D)),
            dma((NC, T)), dma((NC, T)),
            dma((NC, T)), dma((NC, T)),
            dma((NC,)), dma((NC,)),
            dma((NC, T // 4)), dma((NC, T // 4)),
            dma((NC,)), dma((NC,)),
            dma((NC, D)), dma((NC, D)),
            dma((D // 2,)), dma((D // 2,)), dma((1,)), dma((1,)),
            dma((D // 2,)), dma((D // 2,)), dma((1,)), dma((1,)),
            dma((D // 2,)), dma((D // 2,)), dma((1,)), dma((1,)),
            dma((T,)), dma((T,)),
            dma((D,)), dma((D,)),
        ],
        compiler_params=pltpu.CompilerParams(
            collective_id=0, has_side_effects=True, vmem_limit_bytes=60 << 20
        ),
    )(
        embeddings.reshape(T, D, SB, OC), tower_v[0], tower_u[0], cross_bias, proj_w[0], proj_bias,
        arch_v, arch_u, arch_bias[None], logit_w[None], labels[None],
    )
    n = len(outs)
    eg, vw, uw, cb, pw, pb, gav, gau, gab, glw = pl.pallas_call(
        functools.partial(deliver, n),
        out_shape=tuple(jax.ShapeDtypeStruct(x.shape, x.dtype) for x in outs),
        in_specs=[hbm] * n,
        out_specs=(hbm,) * n,
        scratch_shapes=[pltpu.VMEM(x.shape, x.dtype) for x in outs]
        + [dma((T + n - 1,)), dma((T + n - 1,))],
        compiler_params=pltpu.CompilerParams(vmem_limit_bytes=60 << 20),
    )(*outs)
    return (
        eg.reshape(rows, OC), vw[None], uw[None], cb, pw[None], pb,
        gav, gau, gab[0], glw[0],
    )


def solution(mesh):
    return jax.shard_map(
        local,
        mesh=mesh,
        in_specs=(
            P(None, ("tower", "dev")),
            P("tower", None, None),
            P("tower", None, None),
            P("tower", None),
            P("tower", None, None),
            P("tower", None),
            P(),
            P(),
            P(),
            P(),
            P(("tower", "dev")),
        ),
        out_specs=(
            P(None, ("tower", "dev")),
            P("tower", "dev", None),
            P("tower", "dev", None),
            P("tower", "dev"),
            P("tower", "dev", None),
            P("tower", "dev"),
            P(("tower", "dev"), None),
            P(("tower", "dev"), None),
            P(("tower", "dev")),
            P(("tower", "dev")),
        ),
        check_vma=False,
    )
```
